256 devices in a mesh: dp: 8 (over x_hi, y), group: 2 (over x_lo), seq: 16 (over z, core).
Axes of the slice: x: 4 (x_hi: 2, x_lo: 2; x = x_hi * 2 + x_lo), y: 4, z: 8, core: 2. Of those that a mesh axis runs over, the one named last changes fastest.
Arguments:
- student_hidden: bfloat16 [8, 1280, 5120], P('dp', 'seq'), may hold values from -6 to 6
- student_mod: float32 [2, 5120], replicated, may hold values from -3 to 3
- student_out: bfloat16 [5120, 64], replicated, may hold values from -0.078125 to 0.078125
- score_stream: bfloat16 [2, 8, 1280, 5120], P('group', 'dp', 'seq')
- score_in: bfloat16 [2, 64, 5120], P('group'), may hold values from -0.75 to 0.75
- score_mod: float32 [2, 16, 2, 5120], P('group'), may hold values from -3 to 3
- attention_in: bfloat16 [2, 5120, 3, 4096], P('group', None, None, 'seq')
- head_out: bfloat16 [2, 32, 128, 64], P('group', 'seq'), may hold values from -6 to 6
- step_index: int32 [8], P('dp'), may hold values from 0 to 15
- lengths: int32 [8], P('dp'), may hold values from 1 to 1280, 6400 in all
- noise: bfloat16 [8, 64, 1280], P('dp', None, 'seq'), may hold values from -6 to 6
Outputs:
- latent_gradient: float32 [8, 64, 1280], P('dp', 'group', 'seq')
The draws below stay inside these ranges and needn't reach their ends.
Inputs may be any that keep to these rules, and one draw needn't show every extreme that they name: `lengths`: one sample in every draw has all 1280 tokens valid.
All inputs are finite; a program needn't handle non-finite values. No bound on the sum of `lengths` on one device may be relied on, other than what follows from the above.
Results may differ from the reference program's by a relative error of at most 0.0045.
Values may be sent and summed in bfloat16 or wider, within the bound.
No kernel may reach another device: no remote copies, remote signals or barrier semaphores. Data moves between devices by JAX's collectives and lax.ppermute only.
A program may use at most 128 MiB of HBM per device.

```python
import math
import jax
import jax.numpy as jnp
import numpy as np
from jax import lax

D = 5120
HEADS = 32
HS = 128
PATCH = 64
LEVELS = 16
TOKENS = 1280
SAMPLES = 8
N_DP = 8


def draw_attention_in(key, part):
    key = jax.random.fold_in(key, 7)
    base_key = jax.random.fold_in(key, 0)
    weights = jax.random.normal(base_key, (2, D, 3, HEADS, HS), jnp.float32) * D ** (-0.5)
    return weights.reshape(2, D, 3, HEADS * HS).astype(jnp.bfloat16)


def draw_score_stream(key, part):
    key = jax.random.fold_in(key, 11)
    value_key, row_key, column_key = jax.random.split(key, 3)
    shape = (2, SAMPLES, TOKENS, D)
    row_scale = jnp.exp(jax.random.uniform(row_key, (2, SAMPLES, TOKENS, 1), jnp.float32, -1.2, 1.1))
    column_scale = jnp.exp(jax.random.uniform(column_key, (2, 1, 1, D), jnp.float32, -1.2, 1.1))
    values = jax.random.normal(value_key, shape, jnp.float32)
    return (values * row_scale * column_scale).astype(jnp.bfloat16)


def set_ends(result, stream_key, least, largest):
    place = [jax.random.randint(jax.random.fold_in(stream_key, axis), (), 0, length) for axis, length in enumerate(result.shape)]
    widest = result.shape.index(max(result.shape))
    neighbour = place[:widest] + [(place[widest] + 1) % result.shape[widest]] + place[widest + 1:]
    return result.at[tuple(place)].set(least).at[tuple(neighbour)].set(largest)


def steps_of(own_key, extent, pieces, least, largest):
    loudness = 1.0
    for dim, shards_of in pieces:
        steps = jax.random.uniform(jax.random.fold_in(jax.random.fold_in(own_key, 6), dim), (shards_of,), jnp.float32, least / len(pieces), largest / len(pieces))
        loudness = loudness * jnp.repeat(jnp.exp(steps), extent[dim] // shards_of).reshape((-1,) + (1,) * (len(extent) - 1 - dim))
    return loudness


def split_up(number_of, total, most, skew):
    weights = [(1 << 20) // math.isqrt(rank ** skew) + 1 for rank in range(2, number_of + 1)]
    surplus, holding = total - most - (number_of - 1), [1] * (number_of - 1)
    while surplus > 0:
        candidates = [i for i in range(number_of - 1) if holding[i] < most]
        pool, remaining = sum([weights[i] for i in candidates]), surplus
        for i in candidates:
            extra = min(most - holding[i], max(1, remaining * weights[i] // pool), surplus)
            holding[i] = holding[i] + extra
            surplus = surplus - extra
    return np.array([most] + holding)


def ragged_sizes(stream_key, number_of, total, reach, slope):
    if number_of == 2:
        one = jax.random.randint(stream_key, (), max(1, total - reach), min(reach, total - 1) + 1)
        return jnp.stack([one, total - one])
    sizes = jnp.asarray(split_up(number_of, total, reach, slope), jnp.int32)
    couples = (number_of - 1) // 2
    donor, receiver = sizes[1:1 + 2 * couples:2], sizes[2:2 + 2 * couples:2]
    room = jnp.minimum(donor - 1, reach - receiver)
    passed = jax.random.randint(jax.random.fold_in(stream_key, 1), (couples,), 0, 1 << 20) % (room + 1)
    sizes = sizes.at[1:1 + 2 * couples:2].set(donor - passed).at[2:2 + 2 * couples:2].set(receiver + passed)
    return sizes[jax.random.permutation(jax.random.fold_in(stream_key, 2), number_of)]


def bell_draw(own_key, shape, spread, bound, cuts=(), kind=jnp.bfloat16):
    values = jax.random.normal(own_key, shape, jnp.float32) * spread
    if len(cuts) > 0:
        values = steps_of(own_key, shape, cuts, -0.22, 0.18) * values
    return jnp.clip(values, min=-bound, max=bound).astype(kind)


def setup_inputs(seed: int = 0) -> dict:
    key_of = jax.random.split(jax.random.key(seed), 12)
    student_hidden = bell_draw(key_of[0], (SAMPLES, TOKENS, D), 1.0, 6.0, ((0, 8), (1, 16)))
    student_mod = bell_draw(key_of[1], (2, D), 0.5, 3.0, (), jnp.float32)
    student_out = bell_draw(key_of[2], (D, PATCH), D ** -0.5, 0.078125)
    score_stream = draw_score_stream(jax.random.fold_in(key_of[11], 71), 0)
    score_in = bell_draw(key_of[4], (2, PATCH, D), PATCH ** -0.5, 0.75, ((0, 2),))
    score_mod = bell_draw(key_of[5], (2, LEVELS, 2, D), 0.5, 3.0, ((0, 2),), jnp.float32)
    attention_in = draw_attention_in(jax.random.fold_in(key_of[11], 71), 0)
    head_out = bell_draw(key_of[7], (2, HEADS, HS, PATCH), ((TOKENS / (HEADS * HS)) ** 0.5), 6.0, ((0, 2), (1, 16)))
    step_index = set_ends(jax.random.randint(key_of[8], (SAMPLES,), 0, LEVELS), jax.random.fold_in(key_of[8], 1), 0, LEVELS - 1).astype(jnp.int32)
    lengths = ragged_sizes(key_of[9], SAMPLES, TOKENS * N_DP * 5 // 8, TOKENS, 2).astype(jnp.int32)
    noise = bell_draw(key_of[10], (SAMPLES, PATCH, TOKENS), 1.0, 6.0, ((0, 8), (2, 16)))
    return {"student_hidden": student_hidden, "student_mod": student_mod, "student_out": student_out, "score_stream": score_stream, "score_in": score_in, "score_mod": score_mod, "attention_in": attention_in, "head_out": head_out, "step_index": step_index, "lengths": lengths, "noise": noise}


epsilon = 1e-06

def layer_norm(values):
    average = lax.optimization_barrier(jnp.mean(values, -1, keepdims=True))
    centered = values - average
    variance = lax.optimization_barrier(jnp.mean(centered * centered, -1, keepdims=True))
    return centered * lax.rsqrt(variance + epsilon)

def model_output(noised, stream, valid, selected, embed_weight, mod_table, projection, head_weights):
    modulation = lax.optimization_barrier(jnp.sum(jnp.where(selected[:, None, None], mod_table, 0.0), 0))
    embedded = stream.astype(jnp.float32) + jnp.dot(noised, embed_weight, preferred_element_type=jnp.float32)
    normed = (layer_norm(embedded) * (1.0 + modulation[1]) + modulation[0]).astype(jnp.bfloat16)
    projected = jnp.dot(normed, projection.reshape(D, 3 * HEADS * HS), preferred_element_type=jnp.float32).astype(jnp.bfloat16)
    projected = projected.reshape(TOKENS, 3, HEADS, HS).transpose(1, 2, 0, 3)

    def one_head(operands):
        queries, key_rows, value_rows, head_weight = operands
        scores = jnp.dot(queries, key_rows.T, preferred_element_type=jnp.float32) * HS ** (-0.5)
        scores = jnp.where(valid[None, :], scores, -1e+30)
        highest = lax.optimization_barrier(jnp.max(scores, -1, keepdims=True))
        lifted = jnp.exp(scores - highest)
        chances = (lifted / lax.optimization_barrier(jnp.sum(lifted, -1, keepdims=True))).astype(jnp.bfloat16)
        mixture = jnp.dot(chances, value_rows, preferred_element_type=jnp.float32).astype(jnp.bfloat16)
        return jnp.dot(mixture, head_weight, preferred_element_type=jnp.float32)
    return lax.optimization_barrier(jnp.sum(lax.map(one_head, (projected[0], projected[1], projected[2], head_weights)), 0))

def reference(student_hidden, student_mod, student_out, score_stream, score_in, score_mod, attention_in, head_out, step_index, lengths, noise):

    def one_sample(operands):
        hidden, teacher_stream, faker_stream, noise_rows, step_now, length = operands
        normed = (layer_norm(hidden.astype(jnp.float32)) * (1.0 + student_mod[1]) + student_mod[0]).astype(jnp.bfloat16)
        latent = jnp.dot(normed, student_out, preferred_element_type=jnp.float32)
        noise_level = (step_now.astype(jnp.float32) + 1.0) / (LEVELS + 1.0)
        noised = ((1.0 - noise_level) * latent + noise_level * noise_rows.T.astype(jnp.float32)).astype(jnp.bfloat16)
        valid = jnp.arange(TOKENS, dtype=jnp.int32) < length
        selected = jnp.arange(LEVELS, dtype=jnp.int32) == step_now
        teacher = model_output(noised, teacher_stream, valid, selected, score_in[0], score_mod[0], attention_in[0], head_out[0])
        faker = model_output(noised, faker_stream, valid, selected, score_in[1], score_mod[1], attention_in[1], head_out[1])
        return jnp.where(valid[:, None], teacher - faker, 0.0).T
    return lax.map(one_sample, (student_hidden, score_stream[0], score_stream[1], noise, step_index, lengths))
```

```python
import functools

import jax
import jax.numpy as jnp
from jax import lax
from jax.experimental import pallas as pl
from jax.experimental.pallas import tpu as pltpu
from jax.sharding import PartitionSpec as P

epsilon = 1e-06
LOG2E = 1.4426950408889634
MIB = 1 << 20
NT = (((1,), (1,)), ((), ()))
TN = (((0,), (0,)), ((), ()))
NN = (((1,), (0,)), ((), ()))


def dot(a, b, dims):
    return lax.dot_general(a, b, dims, preferred_element_type=jnp.float32)


def layer_norm(values):
    average = jnp.mean(values, -1, keepdims=True)
    centered = values - average
    variance = jnp.mean(centered * centered, -1, keepdims=True)
    return centered * lax.rsqrt(variance + epsilon)


def own_rows_kernel(
    step_ref, hidden_ref, mod_ref, out_ref, noise_ref, stream_ref, embed_ref, table_ref, normed_ref, *, levels
):
    mod = mod_ref[...]
    student = (
        layer_norm(hidden_ref[...].astype(jnp.float32)) * (1.0 + mod[1:2]) + mod[0:1]
    ).astype(jnp.bfloat16)
    latent = dot(out_ref[...], student, NT)
    step = jnp.full(latent.shape, step_ref[0], jnp.int32).astype(jnp.float32)
    level = (step + 1.0) / (levels + 1.0)
    noised = ((1.0 - level) * latent + level * noise_ref[...].astype(jnp.float32)).astype(jnp.bfloat16)
    embedded = stream_ref[...].astype(jnp.float32) + dot(noised, embed_ref[...], TN)
    table = table_ref[0]
    normed_ref[...] = (layer_norm(embedded) * (1.0 + table[1:2]) + table[0:1]).astype(jnp.bfloat16)


def own_rows(step, hidden, mod, out_t, noise, stream, embed, table):
    rows, width = hidden.shape
    levels = table.shape[0]

    def whole(x):
        return pl.BlockSpec(x.shape, lambda i, s: (0,) * x.ndim)

    return pl.pallas_call(
        functools.partial(own_rows_kernel, levels=levels),
        grid_spec=pltpu.PrefetchScalarGridSpec(
            num_scalar_prefetch=1,
            grid=(1,),
            in_specs=[whole(x) for x in (hidden, mod, out_t, noise, stream, embed)]
            + [pl.BlockSpec((1, 2, width), lambda i, s: (s[0], 0, 0))],
            out_specs=pl.BlockSpec((rows, width), lambda i, s: (0, 0)),
        ),
        out_shape=jax.ShapeDtypeStruct((rows, width), jnp.bfloat16),
        compiler_params=pltpu.CompilerParams(vmem_limit_bytes=40 * MIB),
        cost_estimate=pl.CostEstimate(flops=2 * 10**8, bytes_accessed=5 * 10**6, transcendentals=0),
        name="own_rows",
    )(step, hidden, mod, out_t, noise, stream, embed, table)


def project_kernel(*refs, blocks, rows):
    x_refs = refs[:blocks]
    wa_ref, wb_ref, q_ref, kv_ref, x_buf, w_buf, x_sem, w_sem = refs[blocks:]
    x_copies = [
        pltpu.make_async_copy(x_refs[i], x_buf.at[pl.ds(i * rows, rows)], x_sem.at[i]) for i in range(blocks)
    ]
    w_copies = []
    for n in range(6):
        source = wa_ref if n < 3 else wb_ref
        w_copies.append(pltpu.make_async_copy(source.at[n % 3], w_buf.at[n], w_sem.at[n]))
    for copy in x_copies + w_copies:
        copy.start()
    for copy in x_copies:
        copy.wait()
    for n in range(6):
        w_copies[n].wait()
        value = dot(x_buf[...], w_buf[n], NN).astype(jnp.bfloat16)
        pair, kind = n // 3, n % 3
        if kind == 0:
            q_ref[pair] = value
        else:
            kv_ref[2 * pair + kind - 1] = value


def project(xs, wa, wb):
    blocks = len(xs)
    rows, width = xs[0].shape
    columns = wa.shape[2]
    total = blocks * rows
    return pl.pallas_call(
        functools.partial(project_kernel, blocks=blocks, rows=rows),
        in_specs=[pl.BlockSpec(memory_space=pl.ANY)] * (blocks + 2),
        out_specs=[pl.BlockSpec(memory_space=pltpu.VMEM)] * 2,
        out_shape=[
            jax.ShapeDtypeStruct((2, total, columns), jnp.bfloat16),
            jax.ShapeDtypeStruct((4, total, columns), jnp.bfloat16),
        ],
        scratch_shapes=[
            pltpu.VMEM((total, width), jnp.bfloat16),
            pltpu.VMEM((6, width, columns), jnp.bfloat16),
            pltpu.SemaphoreType.DMA((blocks,)),
            pltpu.SemaphoreType.DMA((6,)),
        ],
        compiler_params=pltpu.CompilerParams(vmem_limit_bytes=40 * MIB),
        cost_estimate=pl.CostEstimate(
            flops=2 * total * width * 6 * columns,
            bytes_accessed=12 * width * columns + 2 * total * width,
            transcendentals=0,
        ),
        name="project_rows",
    )(*xs, wa, wb)


def attend_kernel(
    place_ref, bias_ref, ha_ref, hb_ref, *refs, calls, rows, sizes, head_size, scale
):
    q_refs = refs[:calls]
    own_refs = refs[calls : 2 * calls]
    far_refs = refs[2 * calls : 3 * calls]
    out_ref, q_buf, k_buf, v_buf, mix = refs[3 * calls :]
    own = sum(sizes)
    at = 0
    for i, size in enumerate(sizes):
        for pair in range(2):
            q_buf[pair, pl.ds(at, size)] = q_refs[i][pair]
            k_buf[pair, pl.ds(at, size)] = own_refs[i][2 * pair]
            v_buf[pair, pl.ds(at, size)] = own_refs[i][2 * pair + 1]
            k_buf[pair, pl.ds(own + at, size)] = far_refs[i][2 * (1 - pair)]
            v_buf[pair, pl.ds(own + at, size)] = far_refs[i][2 * (1 - pair) + 1]
        at += size
    chunk = 160

    @pl.loop(0, own // chunk)
    def _(step):
        here = pl.ds(pl.multiple_of(step * chunk, chunk), chunk)
        bias = bias_ref[...]
        for pair in range(2):
            for sub in range(2):
                lanes = pl.ds(sub * head_size, head_size)
                scores = dot(q_buf[pair, here, lanes], k_buf[pair, :, lanes], NT) * scale + bias
                highest = jnp.max(scores, -1, keepdims=True)
                lifted = jnp.exp2(scores - highest)
                total = jnp.sum(lifted, -1, keepdims=True)
                mixed = dot(lifted.astype(jnp.bfloat16), v_buf[pair, :, lanes], NN) / total
                mix[here, pl.ds((2 * pair + sub) * head_size, head_size)] = mixed.astype(jnp.bfloat16)

    half = out_ref.shape[2]
    for j in range(own // rows):
        result = None
        for n in range(4):
            head_ref = ha_ref if n < 2 else hb_ref
            term = dot(head_ref[n % 2], mix[pl.ds(j * rows, rows), pl.ds(n * head_size, head_size)], NT)
            result = term if result is None else result + term
        out_ref[0, place_ref[j]] = result[:half]
        out_ref[1, place_ref[j]] = result[half:]


def attend(place, bias, ha, hb, qs, owns, fars, rows, groups, head_size):
    calls = len(qs)
    sizes = tuple(q.shape[1] for q in qs)
    own = sum(sizes)
    columns = qs[0].shape[2]
    patch = ha.shape[1]
    blocks = own // rows
    vmem = pl.BlockSpec(memory_space=pltpu.VMEM)
    return pl.pallas_call(
        functools.partial(
            attend_kernel,
            calls=calls,
            rows=rows,
            sizes=sizes,
            head_size=head_size,
            scale=head_size ** (-0.5) * LOG2E,
        ),
        in_specs=[pl.BlockSpec(memory_space=pltpu.SMEM)] + [vmem] * (3 + 3 * calls),
        out_specs=vmem,
        out_shape=jax.ShapeDtypeStruct((groups, blocks, patch // groups, rows), jnp.float32),
        scratch_shapes=[
            pltpu.VMEM((2, own, columns), jnp.bfloat16),
            pltpu.VMEM((2, 2 * own, columns), jnp.bfloat16),
            pltpu.VMEM((2, 2 * own, columns), jnp.bfloat16),
            pltpu.VMEM((own, 2 * columns), jnp.bfloat16),
        ],
        compiler_params=pltpu.CompilerParams(vmem_limit_bytes=40 * MIB),
        cost_estimate=pl.CostEstimate(
            flops=16 * own * own * columns, bytes_accessed=10**7, transcendentals=8 * own * own
        ),
        name="attend",
    )(place, bias, ha, hb, *qs, *owns, *fars)


def local(
    student_hidden,
    student_mod,
    student_out,
    score_stream,
    score_in,
    score_mod,
    attention_in,
    head_out,
    step_index,
    lengths,
    noise,
):
    groups = lax.axis_size("group")
    seq_count = lax.axis_size("seq")
    chips = seq_count // 2
    seq_at = lax.axis_index("seq")
    chip_at, core_at = seq_at // 2, seq_at % 2
    rows = student_hidden.shape[1]
    head_size = head_out.shape[2]
    length = lengths[0]

    def hop(block, sign):
        route = []
        for z in range(chips):
            for core in range(2):
                way = sign if core == 0 else -sign
                route.append((2 * z + core, 2 * ((z + way) % chips) + core))
        return lax.ppermute(block, "seq", route)

    def other_core(block):
        return lax.ppermute(block, "seq", [(i, i ^ 1) for i in range(seq_count)])

    normed = own_rows(
        step_index,
        student_hidden[0],
        student_mod,
        student_out.T,
        noise[0],
        score_stream[0, 0],
        score_in[0],
        score_mod[0],
    )
    wa = attention_in[0].transpose(1, 0, 2)
    ha = head_out[0].transpose(0, 2, 1)

    up = [hop(normed, 1)]
    down = [hop(normed, -1)]
    wb = other_core(wa)
    hb = other_core(ha)
    for _ in range(chips // 2 - 2):
        up.append(hop(up[-1], 1))
        down.append(hop(down[-1], -1))
    up.append(hop(up[-1], 1))

    sets = [[normed, up[0], down[0]]] + [[up[k], down[k]] for k in range(1, chips // 2 - 1)] + [[up[-1]]]
    qs, owns, fars = [], [], []
    for xs in sets:
        q, kv = project(xs, wa, wb)
        qs.append(q)
        owns.append(kv)
        fars.append(other_core(kv))

    order = [0]
    for k in range(1, chips // 2):
        order += [-k, k]
    order.append(-(chips // 2))
    apart = jnp.asarray(order, jnp.int32)

    def places(core):
        return (chip_at + jnp.where(core == 0, apart, -apart)) % chips

    def bias_of(core):
        tokens = (places(core) * 2 + core)[:, None] * rows + jnp.arange(rows, dtype=jnp.int32)
        return jnp.where(tokens < length, 0.0, -1e30).reshape(1, chips * rows)

    bias = jnp.concatenate([bias_of(core_at), bias_of(1 - core_at)], 1)
    terms = attend(places(core_at), bias, ha, hb, qs, owns, fars, rows, groups, head_size)

    half = terms.shape[2]
    terms = terms.reshape(groups * chips, half, rows)
    same_core = [[g * seq_count + 2 * z + c for g in range(groups) for z in range(chips)] for c in range(2)]
    terms = lax.all_to_all(terms, ("group", "seq"), 0, 0, axis_index_groups=same_core, tiled=True)
    terms = terms.reshape(groups, chips, half, rows)
    gradient = jnp.sum(terms[0], 0) - jnp.sum(terms[1], 0)
    own_places = seq_at * rows + jnp.arange(rows, dtype=jnp.int32)
    return jnp.where((own_places < length)[None, :], gradient, 0.0)[None]


def solution(mesh):
    return jax.shard_map(
        local,
        mesh=mesh,
        in_specs=(
            P("dp", "seq", None),
            P(),
            P(),
            P("group", "dp", "seq", None),
            P("group", None, None),
            P("group", None, None, None),
            P("group", None, None, "seq"),
            P("group", "seq", None, None),
            P("dp"),
            P("dp"),
            P("dp", None, "seq"),
        ),
        out_specs=P("dp", "group", "seq"),
        check_vma=False,
    )
```

```python
import functools

import jax
import jax.numpy as jnp
from jax import lax
from jax.experimental import pallas as pl
from jax.experimental.pallas import tpu as pltpu
from jax.sharding import PartitionSpec as P

epsilon = 1e-06
LOG2E = 1.4426950408889634
MIB = 1 << 20
NT = (((1,), (1,)), ((), ()))
TN = (((0,), (0,)), ((), ()))
NN = (((1,), (0,)), ((), ()))


def dot(a, b, dims):
    return lax.dot_general(a, b, dims, preferred_element_type=jnp.float32)


def layer_norm(values):
    average = jnp.mean(values, -1, keepdims=True)
    centered = values - average
    variance = jnp.mean(centered * centered, -1, keepdims=True)
    return centered * lax.rsqrt(variance + epsilon)


def own_rows_kernel(
    step_ref, hidden_any, mod_any, out_any, noise_any, stream_any, embed_any, table_any, *refs, levels, cuts
):
    normed_refs = refs[: len(cuts)]
    hidden_ref, mod_ref, out_ref, noise_ref, stream_ref, embed_ref, table_ref, sems = refs[len(cuts) :]
    pairs = [
        (hidden_any, hidden_ref),
        (mod_any, mod_ref),
        (out_any, out_ref),
        (noise_any, noise_ref),
        (stream_any, stream_ref),
        (embed_any, embed_ref),
        (table_any.at[step_ref[0]], table_ref),
    ]
    copies = [pltpu.make_async_copy(a, b, sems.at[i]) for i, (a, b) in enumerate(pairs)]
    for copy in copies:
        copy.start()
    copies[0].wait()
    copies[1].wait()
    mod = mod_ref[...]
    student = (
        layer_norm(hidden_ref[...].astype(jnp.float32)) * (1.0 + mod[1:2]) + mod[0:1]
    ).astype(jnp.bfloat16)
    copies[2].wait()
    latent = dot(out_ref[...], student, NT)
    step = jnp.full(latent.shape, step_ref[0], jnp.int32).astype(jnp.float32)
    level = (step + 1.0) / (levels + 1.0)
    copies[3].wait()
    noised = ((1.0 - level) * latent + level * noise_ref[...].astype(jnp.float32)).astype(jnp.bfloat16)
    for copy in copies[4:]:
        copy.wait()
    embedded = stream_ref[...].astype(jnp.float32) + dot(noised, embed_ref[...], TN)
    table = table_ref[...]
    normed = (layer_norm(embedded) * (1.0 + table[1:2]) + table[0:1]).astype(jnp.bfloat16)
    at = 0
    for ref, size in zip(normed_refs, cuts):
        ref[...] = normed[at : at + size]
        at += size


def own_rows(step, hidden, mod, out_t, noise, stream, embed, table, cuts):
    width = hidden.shape[1]
    levels = table.shape[0]
    arrays = (hidden, mod, out_t, noise, stream, embed)
    return pl.pallas_call(
        functools.partial(own_rows_kernel, levels=levels, cuts=cuts),
        in_specs=[pl.BlockSpec(memory_space=pltpu.SMEM)] + [pl.BlockSpec(memory_space=pl.ANY)] * 7,
        out_specs=[pl.BlockSpec(memory_space=pltpu.VMEM)] * len(cuts),
        out_shape=[jax.ShapeDtypeStruct((size, width), jnp.bfloat16) for size in cuts],
        scratch_shapes=[pltpu.VMEM(x.shape, x.dtype) for x in arrays]
        + [pltpu.VMEM((2, width), jnp.float32), pltpu.SemaphoreType.DMA((7,))],
        compiler_params=pltpu.CompilerParams(vmem_limit_bytes=58 * MIB),
        cost_estimate=pl.CostEstimate(flops=2 * 10**8, bytes_accessed=5 * 10**6, transcendentals=0),
        name="own_rows",
    )(step, hidden, mod, out_t, noise, stream, embed, table)


def project_kernel(*refs, sizes, fetch, keep, before):
    refs = list(refs)
    x_refs = [refs.pop(0) for _ in sizes]
    w_any = [refs.pop(0) for _ in range(2 if fetch else 1)]
    q_before, kv_before = (refs.pop(0), refs.pop(0)) if before else (None, None)
    q_ref, kv_ref = refs.pop(0), refs.pop(0)
    w_ref = refs.pop(0) if fetch else w_any[0]
    x_buf = refs.pop(0)
    copies = []
    if fetch:
        sems = refs.pop(0)
        copies = [
            pltpu.make_async_copy(w_any[n // 3].at[n % 3], w_ref.at[n], sems.at[n]) for n in range(6)
        ]
        for copy in copies[:3]:
            copy.start()
    at = 0
    for ref, size in zip(x_refs, sizes):
        x_buf[pl.ds(at, size)] = ref[...]
        at += size
    size = q_ref.shape[2]
    if before:
        q_ref[:, pl.ds(0, before)] = q_before[...]
        kv_ref[:, pl.ds(0, before)] = kv_before[...]
    here = pl.ds(before, sum(sizes))
    for n in range(6):
        if fetch:
            copies[n].wait()
            if n + 3 < 6:
                copies[n + 3].start()
        value = dot(x_buf[...], w_ref[n], NN).astype(jnp.bfloat16)
        pair, kind = n // 3, n % 3
        for sub in range(2):
            part = value[:, sub * size : (sub + 1) * size]
            if kind == 0:
                q_ref[2 * pair + sub, here] = part
            else:
                kv_ref[4 * pair + 2 * (kind - 1) + sub, here] = part


def project(xs, weights, head_size, keep=False, earlier=()):
    fetch = len(weights) == 2
    sizes = tuple(x.shape[0] for x in xs)
    width = xs[0].shape[1]
    columns = weights[0].shape[2]
    total = sum(sizes)
    before = earlier[0].shape[1] if earlier else 0
    vmem = pl.BlockSpec(memory_space=pltpu.VMEM)
    out_shape = [
        jax.ShapeDtypeStruct((4, before + total, head_size), jnp.bfloat16),
        jax.ShapeDtypeStruct((8, before + total, head_size), jnp.bfloat16),
    ]
    scratch = [pltpu.VMEM((total, width), jnp.bfloat16)]
    if keep:
        out_shape.append(jax.ShapeDtypeStruct((6, width, columns), jnp.bfloat16))
    elif fetch:
        scratch.insert(0, pltpu.VMEM((6, width, columns), jnp.bfloat16))
    if fetch:
        scratch.append(pltpu.SemaphoreType.DMA((6,)))
    return pl.pallas_call(
        functools.partial(project_kernel, sizes=sizes, fetch=fetch, keep=keep, before=before),
        in_specs=[vmem] * len(xs)
        + [pl.BlockSpec(memory_space=pl.ANY) if fetch else vmem] * len(weights)
        + [vmem] * len(earlier),
        out_specs=[vmem] * len(out_shape),
        out_shape=out_shape,
        scratch_shapes=scratch,
        compiler_params=pltpu.CompilerParams(vmem_limit_bytes=(10 if keep or not fetch else 40) * MIB),
        cost_estimate=pl.CostEstimate(
            flops=2 * total * width * 6 * columns,
            bytes_accessed=12 * width * columns if fetch else 2 * total * width,
            transcendentals=0,
        ),
        name="project_rows",
    )(*xs, *weights, *earlier)


def attend_kernel(place_ref, bias_ref, ha_ref, hb_ref, *refs, calls, rows, sizes, scale):
    q_refs = refs[:calls]
    own_refs = refs[calls : 2 * calls]
    far_refs = refs[2 * calls : 3 * calls]
    out_ref, q_buf, kv_buf, mix, heads, sems = refs[3 * calls :]
    own = sum(sizes)
    size = q_buf.shape[2]
    pairs = []
    at = 0
    for i, count in enumerate(sizes):
        here, there = pl.ds(at, count), pl.ds(own + at, count)
        pairs += [
            (q_refs[i], q_buf.at[:, here]),
            (own_refs[i].at[pl.ds(0, 8)], kv_buf.at[:, here]),
            (far_refs[i].at[pl.ds(4, 4)], kv_buf.at[pl.ds(0, 4), there]),
            (far_refs[i].at[pl.ds(0, 4)], kv_buf.at[pl.ds(4, 4), there]),
        ]
        at += count
    copies = [pltpu.make_async_copy(a, b, sems.at[j]) for j, (a, b) in enumerate(pairs)]
    for copy in copies:
        copy.start()
    for copy in copies:
        copy.wait()
    bias = bias_ref[...]
    for n in range(4):
        key = 4 * (n // 2) + n % 2
        scores = dot(q_buf[n], kv_buf[key], NT) * scale + bias
        highest = jnp.max(scores, -1, keepdims=True)
        lifted = jnp.exp2(scores - highest)
        total = jnp.sum(lifted, -1, keepdims=True)
        mixed = dot(lifted.astype(jnp.bfloat16), kv_buf[key + 2], NN) * (1.0 / total)
        mix[:, pl.ds(n * size, size)] = mixed.astype(jnp.bfloat16)
    for n in range(4):
        heads[:, pl.ds(n * size, size)] = (ha_ref if n < 2 else hb_ref)[n % 2]
    half = out_ref.shape[2]
    for j in range(own // rows):
        result = dot(heads[...], mix[pl.ds(j * rows, rows)], NT)
        out_ref[0, place_ref[j]] = result[:half]
        out_ref[1, place_ref[j]] = result[half:]


def attend(place, bias, ha, hb, qs, owns, fars, rows, groups, scale):
    calls = len(qs)
    sizes = tuple(q.shape[1] for q in qs)
    own = sum(sizes)
    head_size = qs[0].shape[2]
    patch = ha.shape[1]
    vmem = pl.BlockSpec(memory_space=pltpu.VMEM)
    return pl.pallas_call(
        functools.partial(attend_kernel, calls=calls, rows=rows, sizes=sizes, scale=scale),
        in_specs=[pl.BlockSpec(memory_space=pltpu.SMEM), vmem, vmem, vmem]
        + [pl.BlockSpec(memory_space=pl.ANY)] * (3 * calls),
        out_specs=vmem,
        out_shape=jax.ShapeDtypeStruct((groups, own // rows, patch // groups, rows), jnp.float32),
        scratch_shapes=[
            pltpu.VMEM((4, own, head_size), jnp.bfloat16),
            pltpu.VMEM((8, 2 * own, head_size), jnp.bfloat16),
            pltpu.VMEM((own, 4 * head_size), jnp.bfloat16),
            pltpu.VMEM((patch, 4 * head_size), jnp.bfloat16),
            pltpu.SemaphoreType.DMA((4 * calls,)),
        ],
        compiler_params=pltpu.CompilerParams(vmem_limit_bytes=58 * MIB),
        cost_estimate=pl.CostEstimate(
            flops=32 * own * own * head_size, bytes_accessed=10**7, transcendentals=8 * own * own
        ),
        name="attend",
    )(place, bias, ha, hb, *qs, *owns, *fars)


def local(
    student_hidden,
    student_mod,
    student_out,
    score_stream,
    score_in,
    score_mod,
    attention_in,
    head_out,
    step_index,
    lengths,
    noise,
):
    groups = lax.axis_size("group")
    seq_count = lax.axis_size("seq")
    chips = seq_count // 2
    seq_at = lax.axis_index("seq")
    chip_at, core_at = seq_at // 2, seq_at % 2
    rows = student_hidden.shape[1]
    head_size = head_out.shape[2]
    scale = head_size ** (-0.5) * LOG2E
    length = lengths[0]

    def hop(block, sign):
        route = []
        for z in range(chips):
            for core in range(2):
                way = sign if core == 0 else -sign
                route.append((2 * z + core, 2 * ((z + way) % chips) + core))
        return lax.ppermute(block, "seq", route)

    def other_core(block):
        return lax.ppermute(block, "seq", [(i, i ^ 1) for i in range(seq_count)])

    half_way = chips // 2
    apart = [0, -1]
    for k in range(1, half_way):
        apart += [k, -k - 1]
    apart = jnp.asarray(apart, jnp.int32)

    def places(core):
        return (chip_at + jnp.where(core == 0, apart, -apart)) % chips

    def bias_of(core):
        tokens = (places(core) * 2 + core)[:, None] * rows + jnp.arange(rows, dtype=jnp.int32)
        return jnp.where(tokens < length, 0.0, -1e30)

    normed, *_ = own_rows(
        step_index,
        student_hidden[0],
        student_mod,
        student_out.T,
        noise[0],
        score_stream[0, 0],
        score_in[0],
        score_mod[0],
        (rows,),
    )
    wa = attention_in[0].transpose(1, 0, 2)
    ha = head_out[0].transpose(0, 2, 1)

    up, down = [normed], [normed]
    up.append(hop(up[-1], 1))
    begun, _ = lax.optimization_barrier((ha, normed))
    hb = other_core(begun)
    later, fetched, hb = lax.optimization_barrier((normed, wa, hb))
    down.append(hop(later, -1))
    wb = other_core(fetched)
    bias = jnp.concatenate([bias_of(core_at), bias_of(1 - core_at)]).reshape(1, -1)
    up.append(hop(up[-1], 1))

    place = places(core_at)
    qs, owns, fars = [], [], []
    weights, earlier = [wa, wb], ()
    for k in range(half_way):
        nearer, further = down[k], up[k + 1]
        if k + 1 < half_way:
            nearer, down[k + 1] = lax.optimization_barrier((nearer, down[k + 1]))
        if k + 2 < half_way:
            down.append(hop(down[k + 1], -1))
        q, kv, *kept = project(
            [nearer, further], weights, head_size, keep=k == half_way - 2, earlier=earlier
        )
        weights = kept or weights
        if k + 2 <= half_way:
            up[k + 2], q, kv, fars, bias, place = lax.optimization_barrier((up[k + 2], q, kv, fars, bias, place))
        if k + 3 <= half_way:
            up.append(hop(up[k + 2], 1))
        if k == half_way - 2:
            earlier = (q, kv)
        else:
            qs.append(q)
            owns.append(kv)
            fars.append(other_core(kv))
    terms = attend(place, bias, ha, hb, qs, owns, fars, rows, groups, scale)

    half = terms.shape[2]
    terms = terms.reshape(groups * chips, half, rows)
    same_core = [[g * seq_count + 2 * z + c for g in range(groups) for z in range(chips)] for c in range(2)]
    terms = lax.all_to_all(terms, ("group", "seq"), 0, 0, axis_index_groups=same_core, tiled=True)
    terms = terms.reshape(groups, chips, half, rows)
    gradient = jnp.sum(terms[0], 0) - jnp.sum(terms[1], 0)
    own_places = seq_at * rows + jnp.arange(rows, dtype=jnp.int32)
    return jnp.where((own_places < length)[None, :], gradient, 0.0)[None]


def solution(mesh):
    return jax.shard_map(
        local,
        mesh=mesh,
        in_specs=(
            P("dp", "seq", None),
            P(),
            P(),
            P("group", "dp", "seq", None),
            P("group", None, None),
            P("group", None, None, None),
            P("group", None, None, "seq"),
            P("group", "seq", None, None),
            P("dp"),
            P("dp"),
            P("dp", None, "seq"),
        ),
        out_specs=P("dp", "group", "seq"),
        check_vma=False,
    )
```

```python
import functools

import jax
import jax.numpy as jnp
from jax import lax
from jax.experimental import pallas as pl
from jax.experimental.pallas import tpu as pltpu
from jax.sharding import PartitionSpec as P

epsilon = 1e-06
LOG2E = 1.4426950408889634
MIB = 1 << 20
NT = (((1,), (1,)), ((), ()))
TN = (((0,), (0,)), ((), ()))
NN = (((1,), (0,)), ((), ()))


def dot(a, b, dims):
    return lax.dot_general(a, b, dims, preferred_element_type=jnp.float32)


def layer_norm(values):
    average = jnp.mean(values, -1, keepdims=True)
    centered = values - average
    variance = jnp.mean(centered * centered, -1, keepdims=True)
    return centered * lax.rsqrt(variance + epsilon)


def own_rows_kernel(
    step_ref, hidden_any, mod_any, out_any, noise_any, stream_any, embed_any, table_any, *refs, levels, cuts
):
    normed_refs = refs[: len(cuts)]
    hidden_ref, mod_ref, out_ref, noise_ref, stream_ref, embed_ref, table_ref, sems = refs[len(cuts) :]
    pairs = [
        (hidden_any, hidden_ref),
        (mod_any, mod_ref),
        (out_any, out_ref),
        (noise_any, noise_ref),
        (stream_any, stream_ref),
        (embed_any, embed_ref),
        (table_any.at[step_ref[0]], table_ref),
    ]
    copies = [pltpu.make_async_copy(a, b, sems.at[i]) for i, (a, b) in enumerate(pairs)]
    for copy in copies:
        copy.start()
    copies[0].wait()
    copies[1].wait()
    mod = mod_ref[...]
    student = (
        layer_norm(hidden_ref[...].astype(jnp.float32)) * (1.0 + mod[1:2]) + mod[0:1]
    ).astype(jnp.bfloat16)
    copies[2].wait()
    latent = dot(out_ref[...], student, NT)
    step = jnp.full(latent.shape, step_ref[0], jnp.int32).astype(jnp.float32)
    level = (step + 1.0) / (levels + 1.0)
    copies[3].wait()
    noised = ((1.0 - level) * latent + level * noise_ref[...].astype(jnp.float32)).astype(jnp.bfloat16)
    for copy in copies[4:]:
        copy.wait()
    embedded = stream_ref[...].astype(jnp.float32) + dot(noised, embed_ref[...], TN)
    table = table_ref[...]
    normed = (layer_norm(embedded) * (1.0 + table[1:2]) + table[0:1]).astype(jnp.bfloat16)
    at = 0
    for ref, size in zip(normed_refs, cuts):
        ref[...] = normed[at : at + size]
        at += size


def own_rows(step, hidden, mod, out_t, noise, stream, embed, table, cuts):
    width = hidden.shape[1]
    levels = table.shape[0]
    arrays = (hidden, mod, out_t, noise, stream, embed)
    return pl.pallas_call(
        functools.partial(own_rows_kernel, levels=levels, cuts=cuts),
        in_specs=[pl.BlockSpec(memory_space=pltpu.SMEM)] + [pl.BlockSpec(memory_space=pl.ANY)] * 7,
        out_specs=[pl.BlockSpec(memory_space=pltpu.VMEM)] * len(cuts),
        out_shape=[jax.ShapeDtypeStruct((size, width), jnp.bfloat16) for size in cuts],
        scratch_shapes=[pltpu.VMEM(x.shape, x.dtype) for x in arrays]
        + [pltpu.VMEM((2, width), jnp.float32), pltpu.SemaphoreType.DMA((7,))],
        compiler_params=pltpu.CompilerParams(vmem_limit_bytes=58 * MIB),
        cost_estimate=pl.CostEstimate(flops=2 * 10**8, bytes_accessed=5 * 10**6, transcendentals=0),
        name="own_rows",
    )(step, hidden, mod, out_t, noise, stream, embed, table)


def project_first_kernel(x_ref, w_any, q_ref, kv_ref, w_ref, sems):
    copies = [pltpu.make_async_copy(w_any.at[n], w_ref.at[n], sems.at[n]) for n in range(3)]
    for copy in copies:
        copy.start()
    size = q_ref.shape[2]
    for n in range(3):
        copies[n].wait()
        value = dot(x_ref[...], w_ref[n], NN).astype(jnp.bfloat16)
        for sub in range(2):
            part = value[:, sub * size : (sub + 1) * size]
            if n == 0:
                q_ref[sub] = part
            else:
                kv_ref[2 * (n - 1) + sub] = part


def project_first(x, w, head_size):
    rows, width = x.shape
    vmem = pl.BlockSpec(memory_space=pltpu.VMEM)
    return pl.pallas_call(
        project_first_kernel,
        in_specs=[vmem, pl.BlockSpec(memory_space=pl.ANY)],
        out_specs=[vmem] * 2,
        out_shape=[
            jax.ShapeDtypeStruct((2, rows, head_size), jnp.bfloat16),
            jax.ShapeDtypeStruct((4, rows, head_size), jnp.bfloat16),
        ],
        scratch_shapes=[pltpu.VMEM(w.shape, w.dtype), pltpu.SemaphoreType.DMA((3,))],
        compiler_params=pltpu.CompilerParams(vmem_limit_bytes=58 * MIB),
        cost_estimate=pl.CostEstimate(
            flops=6 * rows * width * w.shape[2], bytes_accessed=2 * w.size, transcendentals=0
        ),
        name="project_first",
    )(x, w)


def project_kernel(*refs, sizes, fetch, keep, before, ready):
    refs = list(refs)
    x_refs = [refs.pop(0) for _ in sizes]
    w_any = [refs.pop(0) for _ in range(2 if fetch else 1)]
    q_before, kv_before = (refs.pop(0), refs.pop(0)) if before else (None, None)
    q_done, kv_done = (refs.pop(0), refs.pop(0)) if ready else (None, None)
    q_ref, kv_ref = refs.pop(0), refs.pop(0)
    w_ref = refs.pop(0) if fetch else w_any[0]
    x_buf = refs.pop(0)
    copies, x_copies = [], []
    if fetch:
        sems = refs.pop(0)
        copies = [
            pltpu.make_async_copy(w_any[n // 3].at[n % 3], w_ref.at[n], sems.at[n]) for n in range(6)
        ]
        for copy in copies[:3]:
            copy.start()
    at = 0
    for i, (ref, size) in enumerate(zip(x_refs, sizes)):
        if fetch:
            x_copies.append(pltpu.make_async_copy(ref, x_buf.at[pl.ds(at, size)], sems.at[6 + i]))
            x_copies[-1].start()
        else:
            x_buf[pl.ds(at, size)] = ref[...]
        at += size
    for copy in x_copies:
        copy.wait()
    size = q_ref.shape[2]
    if before:
        q_ref[:, pl.ds(0, before)] = q_before[...]
        kv_ref[:, pl.ds(0, before)] = kv_before[...]
    for n in range(6):
        if fetch:
            copies[n].wait()
            if n + 3 < 6:
                copies[n + 3].start()
        pair, kind = n // 3, n % 3
        skip = sizes[0] if ready and pair == 0 else 0
        here = pl.ds(before + skip, sum(sizes) - skip)
        value = dot(x_buf[pl.ds(skip, sum(sizes) - skip)], w_ref[n], NN).astype(jnp.bfloat16)
        for sub in range(2):
            part = value[:, sub * size : (sub + 1) * size]
            if kind == 0:
                q_ref[2 * pair + sub, here] = part
            else:
                kv_ref[4 * pair + 2 * (kind - 1) + sub, here] = part
    if ready:
        q_ref[0:2, pl.ds(0, sizes[0])] = q_done[...]
        kv_ref[0:4, pl.ds(0, sizes[0])] = kv_done[...]


def project(xs, weights, head_size, keep=False, earlier=(), ready=()):
    fetch = len(weights) == 2
    sizes = tuple(x.shape[0] for x in xs)
    width = xs[0].shape[1]
    columns = weights[0].shape[2]
    total = sum(sizes)
    before = earlier[0].shape[1] if earlier else 0
    vmem = pl.BlockSpec(memory_space=pltpu.VMEM)
    out_shape = [
        jax.ShapeDtypeStruct((4, before + total, head_size), jnp.bfloat16),
        jax.ShapeDtypeStruct((8, before + total, head_size), jnp.bfloat16),
    ]
    scratch = [pltpu.VMEM((total, width), jnp.bfloat16)]
    if keep:
        out_shape.append(jax.ShapeDtypeStruct((6, width, columns), jnp.bfloat16))
    elif fetch:
        scratch.insert(0, pltpu.VMEM((6, width, columns), jnp.bfloat16))
    if fetch:
        scratch.append(pltpu.SemaphoreType.DMA((6 + len(xs),)))
    return pl.pallas_call(
        functools.partial(
            project_kernel, sizes=sizes, fetch=fetch, keep=keep, before=before, ready=bool(ready)
        ),
        in_specs=[pl.BlockSpec(memory_space=pl.ANY) if fetch else vmem] * (len(xs) + len(weights))
        + [vmem] * (len(earlier) + len(ready)),
        out_specs=[vmem] * len(out_shape),
        out_shape=out_shape,
        scratch_shapes=scratch,
        compiler_params=pltpu.CompilerParams(vmem_limit_bytes=(10 if keep or not fetch else 40) * MIB),
        cost_estimate=pl.CostEstimate(
            flops=2 * total * width * 6 * columns,
            bytes_accessed=12 * width * columns if fetch else 2 * total * width,
            transcendentals=0,
        ),
        name="project_rows",
    )(*xs, *weights, *earlier, *ready)


def attend_kernel(place_ref, bias_ref, ha_ref, hb_ref, *refs, calls, rows, sizes, scale):
    q_refs = refs[:calls]
    own_refs = refs[calls : 2 * calls]
    far_refs = refs[2 * calls : 3 * calls]
    out_ref, q_buf, kv_buf, mix, heads, sems = refs[3 * calls :]
    own = sum(sizes)
    size = q_buf.shape[2]
    pairs = [[], []]
    at = 0
    for i, count in enumerate(sizes):
        here, there = pl.ds(at, count), pl.ds(own + at, count)
        pairs[0].append((q_refs[i], q_buf.at[:, here]))
        for pair in range(2):
            mine, theirs = pl.ds(4 * pair, 4), pl.ds(4 - 4 * pair, 4)
            pairs[pair].append((own_refs[i].at[mine], kv_buf.at[mine, here]))
            pairs[pair].append((far_refs[i].at[theirs], kv_buf.at[mine, there]))
        at += count
    copies = [
        [pltpu.make_async_copy(a, b, sems.at[3 * calls * pair + j]) for j, (a, b) in enumerate(pairs[pair])]
        for pair in range(2)
    ]
    for copy in copies[0] + copies[1]:
        copy.start()
    bias = bias_ref[...]
    for n in range(4):
        if n % 2 == 0:
            for copy in copies[n // 2]:
                copy.wait()
        key = 4 * (n // 2) + n % 2
        scores = dot(q_buf[n], kv_buf[key], NT) * scale + bias
        highest = jnp.max(scores, -1, keepdims=True)
        lifted = jnp.exp2(scores - highest)
        total = jnp.sum(lifted, -1, keepdims=True)
        mixed = dot(lifted.astype(jnp.bfloat16), kv_buf[key + 2], NN) * (1.0 / total)
        mix[:, pl.ds(n * size, size)] = mixed.astype(jnp.bfloat16)
    for n in range(4):
        heads[:, pl.ds(n * size, size)] = (ha_ref if n < 2 else hb_ref)[n % 2]
    half = out_ref.shape[2]
    for j in range(own // rows):
        result = dot(heads[...], mix[pl.ds(j * rows, rows)], NT)
        out_ref[0, place_ref[j]] = result[:half]
        out_ref[1, place_ref[j]] = result[half:]


def attend(place, bias, ha, hb, qs, owns, fars, rows, groups, scale):
    calls = len(qs)
    sizes = tuple(q.shape[1] for q in qs)
    own = sum(sizes)
    head_size = qs[0].shape[2]
    patch = ha.shape[1]
    vmem = pl.BlockSpec(memory_space=pltpu.VMEM)
    return pl.pallas_call(
        functools.partial(attend_kernel, calls=calls, rows=rows, sizes=sizes, scale=scale),
        in_specs=[pl.BlockSpec(memory_space=pltpu.SMEM), vmem, vmem, vmem]
        + [pl.BlockSpec(memory_space=pl.ANY)] * (3 * calls),
        out_specs=vmem,
        out_shape=jax.ShapeDtypeStruct((groups, own // rows, patch // groups, rows), jnp.float32),
        scratch_shapes=[
            pltpu.VMEM((4, own, head_size), jnp.bfloat16),
            pltpu.VMEM((8, 2 * own, head_size), jnp.bfloat16),
            pltpu.VMEM((own, 4 * head_size), jnp.bfloat16),
            pltpu.VMEM((patch, 4 * head_size), jnp.bfloat16),
            pltpu.SemaphoreType.DMA((5 * calls,)),
        ],
        compiler_params=pltpu.CompilerParams(vmem_limit_bytes=26 * MIB),
        cost_estimate=pl.CostEstimate(
            flops=32 * own * own * head_size, bytes_accessed=10**7, transcendentals=8 * own * own
        ),
        name="attend",
    )(place, bias, ha, hb, *qs, *owns, *fars)


def local(
    student_hidden,
    student_mod,
    student_out,
    score_stream,
    score_in,
    score_mod,
    attention_in,
    head_out,
    step_index,
    lengths,
    noise,
):
    groups = lax.axis_size("group")
    seq_count = lax.axis_size("seq")
    chips = seq_count // 2
    seq_at = lax.axis_index("seq")
    chip_at, core_at = seq_at // 2, seq_at % 2
    rows = student_hidden.shape[1]
    head_size = head_out.shape[2]
    scale = head_size ** (-0.5) * LOG2E
    length = lengths[0]

    def hop(block, sign):
        route = []
        for z in range(chips):
            for core in range(2):
                way = sign if core == 0 else -sign
                route.append((2 * z + core, 2 * ((z + way) % chips) + core))
        return lax.ppermute(block, "seq", route)

    def other_core(block):
        return lax.ppermute(block, "seq", [(i, i ^ 1) for i in range(seq_count)])

    half_way = chips // 2
    apart = [0, -1]
    for k in range(1, half_way):
        apart += [k, -k - 1]
    apart = jnp.asarray(apart, jnp.int32)

    def places(core):
        return (chip_at + jnp.where(core == 0, apart, -apart)) % chips

    def bias_of(core):
        tokens = (places(core) * 2 + core)[:, None] * rows + jnp.arange(rows, dtype=jnp.int32)
        return jnp.where(tokens < length, 0.0, -1e30)

    normed, *_ = own_rows(
        step_index,
        student_hidden[0],
        student_mod,
        student_out.T,
        noise[0],
        score_stream[0, 0],
        score_in[0],
        score_mod[0],
        (rows,),
    )
    wa = attention_in[0].transpose(1, 0, 2)
    ha = head_out[0].transpose(0, 2, 1)

    up, down = [normed], [normed]
    up.append(hop(up[-1], 1))
    fetched, begun, _ = lax.optimization_barrier((wa, ha, normed))
    wb = other_core(fetched)
    hb = other_core(begun)
    later, *ready = lax.optimization_barrier((normed, *project_first(normed, wa, head_size)))
    down.append(hop(later, -1))
    bias = jnp.concatenate([bias_of(core_at), bias_of(1 - core_at)]).reshape(1, -1)
    up.append(hop(up[-1], 1))

    place = places(core_at)
    qs, owns, fars = [], [], []
    weights, earlier = [wa, wb], ()
    for k in range(half_way):
        nearer, further = down[k], up[k + 1]
        if 0 < k < half_way - 1:
            nearer, down[k + 1] = lax.optimization_barrier((nearer, down[k + 1]))
        if k + 2 < half_way:
            down.append(hop(down[k + 1], -1))
        q, kv, *kept = project(
            [nearer, further], weights, head_size, keep=k == half_way - 2, earlier=earlier, ready=() if k else ready
        )
        weights = kept or weights
        if k + 2 <= half_way:
            up[k + 2], q, kv, fars, bias, place, hb = lax.optimization_barrier(
                (up[k + 2], q, kv, fars, bias, place, hb)
            )
        if k + 3 <= half_way:
            up.append(hop(up[k + 2], 1))
        if k == half_way - 2:
            earlier = (q, kv)
        else:
            qs.append(q)
            owns.append(kv)
            fars.append(other_core(kv))
    terms = attend(place, bias, ha, hb, qs, owns, fars, rows, groups, scale)

    half = terms.shape[2]
    terms = terms.reshape(groups * chips, half, rows)
    same_core = [[g * seq_count + 2 * z + c for g in range(groups) for z in range(chips)] for c in range(2)]
    terms = lax.all_to_all(terms, ("group", "seq"), 0, 0, axis_index_groups=same_core, tiled=True)
    terms = terms.reshape(groups, chips, half, rows)
    gradient = jnp.sum(terms[0], 0) - jnp.sum(terms[1], 0)
    own_places = seq_at * rows + jnp.arange(rows, dtype=jnp.int32)
    return jnp.where((own_places < length)[None, :], gradient, 0.0)[None]


def solution(mesh):
    return jax.shard_map(
        local,
        mesh=mesh,
        in_specs=(
            P("dp", "seq", None),
            P(),
            P(),
            P("group", "dp", "seq", None),
            P("group", None, None),
            P("group", None, None, None),
            P("group", None, None, "seq"),
            P("group", "seq", None, None),
            P("dp"),
            P("dp"),
            P("dp", None, "seq"),
        ),
        out_specs=P("dp", "group", "seq"),
        check_vma=False,
    )
```

```python
import functools

import jax
import jax.numpy as jnp
from jax import lax
from jax.experimental import pallas as pl
from jax.experimental.pallas import tpu as pltpu
from jax.sharding import PartitionSpec as P

epsilon = 1e-06
LOG2E = 1.4426950408889634
MIB = 1 << 20
NT = (((1,), (1,)), ((), ()))
TN = (((0,), (0,)), ((), ()))
NN = (((1,), (0,)), ((), ()))


def dot(a, b, dims):
    return lax.dot_general(a, b, dims, preferred_element_type=jnp.float32)


def layer_norm(values):
    average = jnp.mean(values, -1, keepdims=True)
    centered = values - average
    variance = jnp.mean(centered * centered, -1, keepdims=True)
    return centered * lax.rsqrt(variance + epsilon)


def own_rows_kernel(
    step_ref, hidden_any, mod_any, out_any, noise_any, stream_any, embed_any, table_any, *refs, levels, cuts
):
    normed_refs = refs[: len(cuts)]
    hidden_ref, mod_ref, out_ref, noise_ref, stream_ref, embed_ref, table_ref, sems = refs[len(cuts) :]
    pairs = [
        (hidden_any, hidden_ref),
        (mod_any, mod_ref),
        (out_any, out_ref),
        (noise_any, noise_ref),
        (stream_any, stream_ref),
        (embed_any, embed_ref),
        (table_any.at[step_ref[0]], table_ref),
    ]
    copies = [pltpu.make_async_copy(a, b, sems.at[i]) for i, (a, b) in enumerate(pairs)]
    for copy in copies:
        copy.start()
    copies[0].wait()
    copies[1].wait()
    mod = mod_ref[...]
    student = (
        layer_norm(hidden_ref[...].astype(jnp.float32)) * (1.0 + mod[1:2]) + mod[0:1]
    ).astype(jnp.bfloat16)
    copies[2].wait()
    latent = dot(out_ref[...], student, NT)
    step = jnp.full(latent.shape, step_ref[0], jnp.int32).astype(jnp.float32)
    level = (step + 1.0) / (levels + 1.0)
    copies[3].wait()
    noised = ((1.0 - level) * latent + level * noise_ref[...].astype(jnp.float32)).astype(jnp.bfloat16)
    for copy in copies[4:]:
        copy.wait()
    embedded = stream_ref[...].astype(jnp.float32) + dot(noised, embed_ref[...], TN)
    table = table_ref[...]
    normed = (layer_norm(embedded) * (1.0 + table[1:2]) + table[0:1]).astype(jnp.bfloat16)
    at = 0
    for ref, size in zip(normed_refs, cuts):
        ref[...] = normed[at : at + size]
        at += size


def own_rows(step, hidden, mod, out_t, noise, stream, embed, table, cuts):
    width = hidden.shape[1]
    levels = table.shape[0]
    arrays = (hidden, mod, out_t, noise, stream, embed)
    return pl.pallas_call(
        functools.partial(own_rows_kernel, levels=levels, cuts=cuts),
        in_specs=[pl.BlockSpec(memory_space=pltpu.SMEM)] + [pl.BlockSpec(memory_space=pl.ANY)] * 7,
        out_specs=[pl.BlockSpec(memory_space=pltpu.VMEM)] * len(cuts),
        out_shape=[jax.ShapeDtypeStruct((size, width), jnp.bfloat16) for size in cuts],
        scratch_shapes=[pltpu.VMEM(x.shape, x.dtype) for x in arrays]
        + [pltpu.VMEM((2, width), jnp.float32), pltpu.SemaphoreType.DMA((7,))],
        compiler_params=pltpu.CompilerParams(vmem_limit_bytes=58 * MIB),
        cost_estimate=pl.CostEstimate(flops=2 * 10**8, bytes_accessed=5 * 10**6, transcendentals=0),
        name="own_rows",
    )(step, hidden, mod, out_t, noise, stream, embed, table)


def project_first_kernel(x_ref, w_any, q_ref, kv_ref, w_ref, sems):
    copies = [pltpu.make_async_copy(w_any.at[n], w_ref.at[n], sems.at[n]) for n in range(3)]
    for copy in copies:
        copy.start()
    size = q_ref.shape[2]
    for n in range(3):
        copies[n].wait()
        value = dot(x_ref[...], w_ref[n], NN).astype(jnp.bfloat16)
        for sub in range(2):
            part = value[:, sub * size : (sub + 1) * size]
            if n == 0:
                q_ref[sub] = part
            else:
                kv_ref[2 * (n - 1) + sub] = part


def project_first(x, w, head_size):
    rows, width = x.shape
    vmem = pl.BlockSpec(memory_space=pltpu.VMEM)
    return pl.pallas_call(
        project_first_kernel,
        in_specs=[vmem, pl.BlockSpec(memory_space=pl.ANY)],
        out_specs=[vmem] * 2,
        out_shape=[
            jax.ShapeDtypeStruct((2, rows, head_size), jnp.bfloat16),
            jax.ShapeDtypeStruct((4, rows, head_size), jnp.bfloat16),
        ],
        scratch_shapes=[pltpu.VMEM(w.shape, w.dtype), pltpu.SemaphoreType.DMA((3,))],
        compiler_params=pltpu.CompilerParams(vmem_limit_bytes=58 * MIB),
        cost_estimate=pl.CostEstimate(
            flops=6 * rows * width * w.shape[2], bytes_accessed=2 * w.size, transcendentals=0
        ),
        name="project_first",
    )(x, w)


def project_kernel(*refs, sizes, fetch, keep, before, ready):
    refs = list(refs)
    x_refs = [refs.pop(0) for _ in sizes]
    w_any = [refs.pop(0) for _ in range(2 if fetch else 1)]
    q_before, kv_before = (refs.pop(0), refs.pop(0)) if before else (None, None)
    q_done, kv_done = (refs.pop(0), refs.pop(0)) if ready else (None, None)
    q_ref, kv_ref = refs.pop(0), refs.pop(0)
    w_ref = refs.pop(0) if fetch else w_any[0]
    x_buf = refs.pop(0)
    copies, x_copies = [], []
    if fetch:
        sems = refs.pop(0)
        copies = [
            pltpu.make_async_copy(w_any[n // 3].at[n % 3], w_ref.at[n], sems.at[n]) for n in range(6)
        ]
        for copy in copies[:3]:
            copy.start()
    at = 0
    for i, (ref, size) in enumerate(zip(x_refs, sizes)):
        if fetch:
            x_copies.append(pltpu.make_async_copy(ref, x_buf.at[pl.ds(at, size)], sems.at[6 + i]))
            x_copies[-1].start()
        else:
            x_buf[pl.ds(at, size)] = ref[...]
        at += size
    for copy in x_copies:
        copy.wait()
    size = q_ref.shape[2]
    if before:
        q_ref[:, pl.ds(0, before)] = q_before[...]
        kv_ref[:, pl.ds(0, before)] = kv_before[...]
    for n in range(6):
        if fetch:
            copies[n].wait()
            if n + 3 < 6:
                copies[n + 3].start()
        pair, kind = n // 3, n % 3
        skip = sizes[0] if ready and pair == 0 else 0
        here = pl.ds(before + skip, sum(sizes) - skip)
        value = dot(x_buf[pl.ds(skip, sum(sizes) - skip)], w_ref[n], NN).astype(jnp.bfloat16)
        for sub in range(2):
            part = value[:, sub * size : (sub + 1) * size]
            if kind == 0:
                q_ref[2 * pair + sub, here] = part
            else:
                kv_ref[4 * pair + 2 * (kind - 1) + sub, here] = part
    if ready:
        q_ref[0:2, pl.ds(0, sizes[0])] = q_done[...]
        kv_ref[0:4, pl.ds(0, sizes[0])] = kv_done[...]


def project(xs, weights, head_size, keep=False, earlier=(), ready=()):
    fetch = len(weights) == 2
    sizes = tuple(x.shape[0] for x in xs)
    width = xs[0].shape[1]
    columns = weights[0].shape[2]
    total = sum(sizes)
    before = earlier[0].shape[1] if earlier else 0
    vmem = pl.BlockSpec(memory_space=pltpu.VMEM)
    out_shape = [
        jax.ShapeDtypeStruct((4, before + total, head_size), jnp.bfloat16),
        jax.ShapeDtypeStruct((8, before + total, head_size), jnp.bfloat16),
    ]
    scratch = [pltpu.VMEM((total, width), jnp.bfloat16)]
    if keep:
        out_shape.append(jax.ShapeDtypeStruct((6, width, columns), jnp.bfloat16))
    elif fetch:
        scratch.insert(0, pltpu.VMEM((6, width, columns), jnp.bfloat16))
    if fetch:
        scratch.append(pltpu.SemaphoreType.DMA((6 + len(xs),)))
    return pl.pallas_call(
        functools.partial(
            project_kernel, sizes=sizes, fetch=fetch, keep=keep, before=before, ready=bool(ready)
        ),
        in_specs=[pl.BlockSpec(memory_space=pl.ANY) if fetch else vmem] * (len(xs) + len(weights))
        + [vmem] * (len(earlier) + len(ready)),
        out_specs=[vmem] * len(out_shape),
        out_shape=out_shape,
        scratch_shapes=scratch,
        compiler_params=pltpu.CompilerParams(vmem_limit_bytes=(10 if keep or not fetch else 40) * MIB),
        cost_estimate=pl.CostEstimate(
            flops=2 * total * width * 6 * columns,
            bytes_accessed=12 * width * columns if fetch else 2 * total * width,
            transcendentals=0,
        ),
        name="project_rows",
    )(*xs, *weights, *earlier, *ready)


def attend_kernel(place_ref, bias_ref, ha_ref, hb_ref, *refs, calls, rows, sizes, scale):
    q_refs = refs[:calls]
    own_refs = refs[calls : 2 * calls]
    far_refs = refs[2 * calls : 3 * calls]
    out_ref, q_buf, kv_buf, mix, heads, sems = refs[3 * calls :]
    own = sum(sizes)
    size = q_buf.shape[2]
    pairs = [[], []]
    at = 0
    for i, count in enumerate(sizes):
        here, there = pl.ds(at, count), pl.ds(own + at, count)
        pairs[0].append((q_refs[i], q_buf.at[:, here]))
        for pair in range(2):
            mine, theirs = pl.ds(4 * pair, 4), pl.ds(4 - 4 * pair, 4)
            pairs[pair].append((own_refs[i].at[mine], kv_buf.at[mine, here]))
            pairs[pair].append((far_refs[i].at[theirs], kv_buf.at[mine, there]))
        at += count
    copies = [
        [pltpu.make_async_copy(a, b, sems.at[3 * calls * pair + j]) for j, (a, b) in enumerate(pairs[pair])]
        for pair in range(2)
    ]
    for copy in copies[0] + copies[1]:
        copy.start()
    bias = bias_ref[...]
    for n in range(4):
        if n % 2 == 0:
            for copy in copies[n // 2]:
                copy.wait()
        key = 4 * (n // 2) + n % 2
        scores = dot(q_buf[n], kv_buf[key], NT) * scale + bias
        highest = jnp.max(scores, -1, keepdims=True)
        lifted = jnp.exp2(scores - highest)
        total = jnp.sum(lifted, -1, keepdims=True)
        mixed = dot(lifted.astype(jnp.bfloat16), kv_buf[key + 2], NN) * (1.0 / total)
        mix[:, pl.ds(n * size, size)] = mixed.astype(jnp.bfloat16)
    for n in range(4):
        heads[:, pl.ds(n * size, size)] = (ha_ref if n < 2 else hb_ref)[n % 2]
    half = out_ref.shape[2]
    for j in range(own // rows):
        result = dot(heads[...], mix[pl.ds(j * rows, rows)], NT)
        out_ref[0, place_ref[j]] = result[:half]
        out_ref[1, place_ref[j]] = result[half:]


def attend(place, bias, ha, hb, qs, owns, fars, rows, groups, scale):
    calls = len(qs)
    sizes = tuple(q.shape[1] for q in qs)
    own = sum(sizes)
    head_size = qs[0].shape[2]
    patch = ha.shape[1]
    vmem = pl.BlockSpec(memory_space=pltpu.VMEM)
    return pl.pallas_call(
        functools.partial(attend_kernel, calls=calls, rows=rows, sizes=sizes, scale=scale),
        in_specs=[pl.BlockSpec(memory_space=pltpu.SMEM), vmem, vmem, vmem]
        + [pl.BlockSpec(memory_space=pl.ANY)] * (3 * calls),
        out_specs=vmem,
        out_shape=jax.ShapeDtypeStruct((groups, own // rows, patch // groups, rows), jnp.float32),
        scratch_shapes=[
            pltpu.VMEM((4, own, head_size), jnp.bfloat16),
            pltpu.VMEM((8, 2 * own, head_size), jnp.bfloat16),
            pltpu.VMEM((own, 4 * head_size), jnp.bfloat16),
            pltpu.VMEM((patch, 4 * head_size), jnp.bfloat16),
            pltpu.SemaphoreType.DMA((5 * calls,)),
        ],
        compiler_params=pltpu.CompilerParams(vmem_limit_bytes=26 * MIB),
        cost_estimate=pl.CostEstimate(
            flops=32 * own * own * head_size, bytes_accessed=10**7, transcendentals=8 * own * own
        ),
        name="attend",
    )(place, bias, ha, hb, *qs, *owns, *fars)


def local(
    student_hidden,
    student_mod,
    student_out,
    score_stream,
    score_in,
    score_mod,
    attention_in,
    head_out,
    step_index,
    lengths,
    noise,
):
    groups = lax.axis_size("group")
    seq_count = lax.axis_size("seq")
    chips = seq_count // 2
    seq_at = lax.axis_index("seq")
    chip_at, core_at = seq_at // 2, seq_at % 2
    rows = student_hidden.shape[1]
    head_size = head_out.shape[2]
    scale = head_size ** (-0.5) * LOG2E
    length = lengths[0]

    def hop(block, sign):
        route = []
        for z in range(chips):
            for core in range(2):
                way = sign if core == 0 else -sign
                route.append((2 * z + core, 2 * ((z + way) % chips) + core))
        return lax.ppermute(block, "seq", route)

    def other_core(block):
        return lax.ppermute(block, "seq", [(i, i ^ 1) for i in range(seq_count)])

    half_way = chips // 2
    apart = [0, -1]
    for k in range(1, half_way):
        apart += [k, -k - 1]
    apart = jnp.asarray(apart, jnp.int32)

    def places(core):
        return (chip_at + jnp.where(core == 0, apart, -apart)) % chips

    def bias_of(core):
        tokens = (places(core) * 2 + core)[:, None] * rows + jnp.arange(rows, dtype=jnp.int32)
        return jnp.where(tokens < length, 0.0, -1e30)

    normed, *_ = own_rows(
        step_index,
        student_hidden[0],
        student_mod,
        student_out.T,
        noise[0],
        score_stream[0, 0],
        score_in[0],
        score_mod[0],
        (rows,),
    )
    wa = attention_in[0].transpose(1, 0, 2)
    ha = head_out[0].transpose(0, 2, 1)

    up, down = [normed], [normed]
    up.append(hop(up[-1], 1))
    fetched, begun, _ = lax.optimization_barrier((wa, ha, normed))
    wb = other_core(fetched)
    hb = other_core(begun)
    later, *ready = lax.optimization_barrier((normed, *project_first(normed, wa, head_size)))
    down.append(hop(later, -1))
    bias = jnp.concatenate([bias_of(core_at), bias_of(1 - core_at)]).reshape(1, -1)
    up.append(hop(up[-1], 1))

    place = places(core_at)
    qs, owns, fars = [], [], []
    weights, earlier = [wa, wb], ()
    for k in range(half_way):
        q, kv, *kept = project(
            [down[k], up[k + 1]],
            weights,
            head_size,
            keep=k == half_way - 2,
            earlier=earlier,
            ready=() if k else ready,
        )
        weights = kept or weights
        if k + 2 < half_way:
            down[k + 1], q, kv, fars, bias, place, hb = lax.optimization_barrier(
                (down[k + 1], q, kv, fars, bias, place, hb)
            )
            down.append(hop(down[k + 1], -1))
        elif k + 2 == half_way:
            down[k + 1], q, kv, fars = lax.optimization_barrier((down[k + 1], q, kv, fars))
        if k + 3 <= half_way:
            up.append(hop(up[k + 2], 1))
        if k == half_way - 2:
            earlier = (q, kv)
        else:
            qs.append(q)
            owns.append(kv)
            fars.append(other_core(kv))
    terms = attend(place, bias, ha, hb, qs, owns, fars, rows, groups, scale)

    half = terms.shape[2]
    terms = terms.reshape(groups * chips, half, rows)
    same_core = [[g * seq_count + 2 * z + c for g in range(groups) for z in range(chips)] for c in range(2)]
    terms = lax.all_to_all(terms, ("group", "seq"), 0, 0, axis_index_groups=same_core, tiled=True)
    terms = terms.reshape(groups, chips, half, rows)
    gradient = jnp.sum(terms[0], 0) - jnp.sum(terms[1], 0)
    own_places = seq_at * rows + jnp.arange(rows, dtype=jnp.int32)
    return jnp.where((own_places < length)[None, :], gradient, 0.0)[None]


def solution(mesh):
    return jax.shard_map(
        local,
        mesh=mesh,
        in_specs=(
            P("dp", "seq", None),
            P(),
            P(),
            P("group", "dp", "seq", None),
            P("group", None, None),
            P("group", None, None, None),
            P("group", None, None, "seq"),
            P("group", "seq", None, None),
            P("dp"),
            P("dp"),
            P("dp", None, "seq"),
        ),
        out_specs=P("dp", "group", "seq"),
        check_vma=False,
    )
```

```python
import functools

import jax
import jax.numpy as jnp
from jax import lax
from jax.experimental import pallas as pl
from jax.experimental.pallas import tpu as pltpu
from jax.sharding import PartitionSpec as P

epsilon = 1e-06
LOG2E = 1.4426950408889634
MIB = 1 << 20
NT = (((1,), (1,)), ((), ()))
TN = (((0,), (0,)), ((), ()))
NN = (((1,), (0,)), ((), ()))


def dot(a, b, dims):
    return lax.dot_general(a, b, dims, preferred_element_type=jnp.float32)


def layer_norm(values):
    average = jnp.mean(values, -1, keepdims=True)
    centered = values - average
    variance = jnp.mean(centered * centered, -1, keepdims=True)
    return centered * lax.rsqrt(variance + epsilon)


def own_rows_kernel(
    step_ref, hidden_any, mod_any, out_any, noise_any, stream_any, embed_any, table_any, *refs, levels, cuts
):
    normed_refs = refs[: len(cuts)]
    hidden_ref, mod_ref, out_ref, noise_ref, stream_ref, embed_ref, table_ref, sems = refs[len(cuts) :]
    pairs = [
        (hidden_any, hidden_ref),
        (mod_any, mod_ref),
        (out_any, out_ref),
        (noise_any, noise_ref),
        (stream_any, stream_ref),
        (embed_any, embed_ref),
        (table_any.at[step_ref[0]], table_ref),
    ]
    copies = [pltpu.make_async_copy(a, b, sems.at[i]) for i, (a, b) in enumerate(pairs)]
    for copy in copies:
        copy.start()
    copies[0].wait()
    copies[1].wait()
    mod = mod_ref[...]
    student = (
        layer_norm(hidden_ref[...].astype(jnp.float32)) * (1.0 + mod[1:2]) + mod[0:1]
    ).astype(jnp.bfloat16)
    copies[2].wait()
    latent = dot(out_ref[...], student, NT)
    step = jnp.full(latent.shape, step_ref[0], jnp.int32).astype(jnp.float32)
    level = (step + 1.0) / (levels + 1.0)
    copies[3].wait()
    noised = ((1.0 - level) * latent + level * noise_ref[...].astype(jnp.float32)).astype(jnp.bfloat16)
    for copy in copies[4:]:
        copy.wait()
    embedded = stream_ref[...].astype(jnp.float32) + dot(noised, embed_ref[...], TN)
    table = table_ref[...]
    normed = (layer_norm(embedded) * (1.0 + table[1:2]) + table[0:1]).astype(jnp.bfloat16)
    at = 0
    for ref, size in zip(normed_refs, cuts):
        ref[...] = normed[at : at + size]
        at += size


def own_rows(step, hidden, mod, out_t, noise, stream, embed, table, cuts):
    width = hidden.shape[1]
    levels = table.shape[0]
    arrays = (hidden, mod, out_t, noise, stream, embed)
    return pl.pallas_call(
        functools.partial(own_rows_kernel, levels=levels, cuts=cuts),
        in_specs=[pl.BlockSpec(memory_space=pltpu.SMEM)] + [pl.BlockSpec(memory_space=pl.ANY)] * 7,
        out_specs=[pl.BlockSpec(memory_space=pltpu.VMEM)] * len(cuts),
        out_shape=[jax.ShapeDtypeStruct((size, width), jnp.bfloat16) for size in cuts],
        scratch_shapes=[pltpu.VMEM(x.shape, x.dtype) for x in arrays]
        + [pltpu.VMEM((2, width), jnp.float32), pltpu.SemaphoreType.DMA((7,))],
        compiler_params=pltpu.CompilerParams(vmem_limit_bytes=58 * MIB),
        cost_estimate=pl.CostEstimate(flops=2 * 10**8, bytes_accessed=5 * 10**6, transcendentals=0),
        name="own_rows",
    )(step, hidden, mod, out_t, noise, stream, embed, table)


def project_first_kernel(x_ref, w_any, q_ref, kv_ref, w_ref, sems):
    copies = [pltpu.make_async_copy(w_any.at[n], w_ref.at[n], sems.at[n]) for n in range(3)]
    for copy in copies:
        copy.start()
    size = q_ref.shape[2]
    for n in range(3):
        copies[n].wait()
        value = dot(x_ref[...], w_ref[n], NN).astype(jnp.bfloat16)
        for sub in range(2):
            part = value[:, sub * size : (sub + 1) * size]
            if n == 0:
                q_ref[sub] = part
            else:
                kv_ref[2 * (n - 1) + sub] = part


def project_first(x, w, head_size):
    rows, width = x.shape
    vmem = pl.BlockSpec(memory_space=pltpu.VMEM)
    return pl.pallas_call(
        project_first_kernel,
        in_specs=[vmem, pl.BlockSpec(memory_space=pl.ANY)],
        out_specs=[vmem] * 2,
        out_shape=[
            jax.ShapeDtypeStruct((2, rows, head_size), jnp.bfloat16),
            jax.ShapeDtypeStruct((4, rows, head_size), jnp.bfloat16),
        ],
        scratch_shapes=[pltpu.VMEM(w.shape, w.dtype), pltpu.SemaphoreType.DMA((3,))],
        compiler_params=pltpu.CompilerParams(vmem_limit_bytes=58 * MIB),
        cost_estimate=pl.CostEstimate(
            flops=6 * rows * width * w.shape[2], bytes_accessed=2 * w.size, transcendentals=0
        ),
        name="project_first",
    )(x, w)


def project_kernel(*refs, sizes, fetch, keep, before, ready):
    refs = list(refs)
    x_refs = [refs.pop(0) for _ in sizes]
    w_any = [refs.pop(0) for _ in range(2 if fetch else 1)]
    q_before, kv_before = (refs.pop(0), refs.pop(0)) if before else (None, None)
    q_done, kv_done = (refs.pop(0), refs.pop(0)) if ready else (None, None)
    q_ref, kv_ref = refs.pop(0), refs.pop(0)
    w_ref = refs.pop(0) if fetch else w_any[0]
    x_buf = refs.pop(0)
    copies, x_copies = [], []
    if fetch:
        sems = refs.pop(0)
        copies = [
            pltpu.make_async_copy(w_any[n // 3].at[n % 3], w_ref.at[n], sems.at[n]) for n in range(6)
        ]
        for copy in copies[:3]:
            copy.start()
    at = 0
    for i, (ref, size) in enumerate(zip(x_refs, sizes)):
        if fetch:
            x_copies.append(pltpu.make_async_copy(ref, x_buf.at[pl.ds(at, size)], sems.at[6 + i]))
            x_copies[-1].start()
        else:
            x_buf[pl.ds(at, size)] = ref[...]
        at += size
    for copy in x_copies:
        copy.wait()
    size = q_ref.shape[2]
    if before:
        q_ref[:, pl.ds(0, before)] = q_before[...]
        kv_ref[:, pl.ds(0, before)] = kv_before[...]
    for n in range(6):
        if fetch:
            copies[n].wait()
            if n + 3 < 6:
                copies[n + 3].start()
        pair, kind = n // 3, n % 3
        skip = sizes[0] if ready and pair == 0 else 0
        here = pl.ds(before + skip, sum(sizes) - skip)
        value = dot(x_buf[pl.ds(skip, sum(sizes) - skip)], w_ref[n], NN).astype(jnp.bfloat16)
        for sub in range(2):
            part = value[:, sub * size : (sub + 1) * size]
            if kind == 0:
                q_ref[2 * pair + sub, here] = part
            else:
                kv_ref[4 * pair + 2 * (kind - 1) + sub, here] = part
    if ready:
        q_ref[0:2, pl.ds(0, sizes[0])] = q_done[...]
        kv_ref[0:4, pl.ds(0, sizes[0])] = kv_done[...]


def project(xs, weights, head_size, keep=False, earlier=(), ready=()):
    fetch = len(weights) == 2
    sizes = tuple(x.shape[0] for x in xs)
    width = xs[0].shape[1]
    columns = weights[0].shape[2]
    total = sum(sizes)
    before = earlier[0].shape[1] if earlier else 0
    vmem = pl.BlockSpec(memory_space=pltpu.VMEM)
    out_shape = [
        jax.ShapeDtypeStruct((4, before + total, head_size), jnp.bfloat16),
        jax.ShapeDtypeStruct((8, before + total, head_size), jnp.bfloat16),
    ]
    scratch = [pltpu.VMEM((total, width), jnp.bfloat16)]
    if keep:
        out_shape.append(jax.ShapeDtypeStruct((6, width, columns), jnp.bfloat16))
    elif fetch:
        scratch.insert(0, pltpu.VMEM((6, width, columns), jnp.bfloat16))
    if fetch:
        scratch.append(pltpu.SemaphoreType.DMA((6 + len(xs),)))
    return pl.pallas_call(
        functools.partial(
            project_kernel, sizes=sizes, fetch=fetch, keep=keep, before=before, ready=bool(ready)
        ),
        in_specs=[pl.BlockSpec(memory_space=pl.ANY) if fetch else vmem] * (len(xs) + len(weights))
        + [vmem] * (len(earlier) + len(ready)),
        out_specs=[vmem] * len(out_shape),
        out_shape=out_shape,
        scratch_shapes=scratch,
        compiler_params=pltpu.CompilerParams(vmem_limit_bytes=(10 if keep or not fetch else 40) * MIB),
        cost_estimate=pl.CostEstimate(
            flops=2 * total * width * 6 * columns,
            bytes_accessed=12 * width * columns if fetch else 2 * total * width,
            transcendentals=0,
        ),
        name="project_rows",
    )(*xs, *weights, *earlier, *ready)


def attend_kernel(place_ref, bias_ref, ha_ref, hb_ref, *refs, calls, rows, sizes, scale):
    q_refs = refs[:calls]
    own_refs = refs[calls : 2 * calls]
    far_refs = refs[2 * calls : 3 * calls]
    out_ref, q_buf, kv_buf, mix, heads, sems = refs[3 * calls :]
    own = sum(sizes)
    size = q_buf.shape[2]
    pairs = [[], []]
    at = 0
    for i, count in enumerate(sizes):
        here, there = pl.ds(at, count), pl.ds(own + at, count)
        pairs[0].append((q_refs[i], q_buf.at[:, here]))
        for pair in range(2):
            mine, theirs = pl.ds(4 * pair, 4), pl.ds(4 - 4 * pair, 4)
            pairs[pair].append((own_refs[i].at[mine], kv_buf.at[mine, here]))
            pairs[pair].append((far_refs[i].at[theirs], kv_buf.at[mine, there]))
        at += count
    copies = [
        [pltpu.make_async_copy(a, b, sems.at[3 * calls * pair + j]) for j, (a, b) in enumerate(pairs[pair])]
        for pair in range(2)
    ]
    for copy in copies[0] + copies[1]:
        copy.start()
    bias = bias_ref[...]
    for n in range(4):
        if n % 2 == 0:
            for copy in copies[n // 2]:
                copy.wait()
        key = 4 * (n // 2) + n % 2
        scores = dot(q_buf[n], kv_buf[key], NT) * scale + bias
        highest = jnp.max(scores, -1, keepdims=True)
        lifted = jnp.exp2(scores - highest)
        total = jnp.sum(lifted, -1, keepdims=True)
        mixed = dot(lifted.astype(jnp.bfloat16), kv_buf[key + 2], NN) * (1.0 / total)
        mix[:, pl.ds(n * size, size)] = mixed.astype(jnp.bfloat16)
    for n in range(4):
        heads[:, pl.ds(n * size, size)] = (ha_ref if n < 2 else hb_ref)[n % 2]
    half = out_ref.shape[2]
    for j in range(own // rows):
        result = dot(heads[...], mix[pl.ds(j * rows, rows)], NT)
        out_ref[0, place_ref[j]] = result[:half]
        out_ref[1, place_ref[j]] = result[half:]


def attend(place, bias, ha, hb, qs, owns, fars, rows, groups, scale):
    calls = len(qs)
    sizes = tuple(q.shape[1] for q in qs)
    own = sum(sizes)
    head_size = qs[0].shape[2]
    patch = ha.shape[1]
    vmem = pl.BlockSpec(memory_space=pltpu.VMEM)
    return pl.pallas_call(
        functools.partial(attend_kernel, calls=calls, rows=rows, sizes=sizes, scale=scale),
        in_specs=[pl.BlockSpec(memory_space=pltpu.SMEM), vmem, vmem, vmem]
        + [pl.BlockSpec(memory_space=pl.ANY)] * (3 * calls),
        out_specs=vmem,
        out_shape=jax.ShapeDtypeStruct((groups, own // rows, patch // groups, rows), jnp.float32),
        scratch_shapes=[
            pltpu.VMEM((4, own, head_size), jnp.bfloat16),
            pltpu.VMEM((8, 2 * own, head_size), jnp.bfloat16),
            pltpu.VMEM((own, 4 * head_size), jnp.bfloat16),
            pltpu.VMEM((patch, 4 * head_size), jnp.bfloat16),
            pltpu.SemaphoreType.DMA((5 * calls,)),
        ],
        compiler_params=pltpu.CompilerParams(vmem_limit_bytes=26 * MIB),
        cost_estimate=pl.CostEstimate(
            flops=32 * own * own * head_size, bytes_accessed=10**7, transcendentals=8 * own * own
        ),
        name="attend",
    )(place, bias, ha, hb, *qs, *owns, *fars)


def local(
    student_hidden,
    student_mod,
    student_out,
    score_stream,
    score_in,
    score_mod,
    attention_in,
    head_out,
    step_index,
    lengths,
    noise,
):
    groups = lax.axis_size("group")
    seq_count = lax.axis_size("seq")
    chips = seq_count // 2
    seq_at = lax.axis_index("seq")
    chip_at, core_at = seq_at // 2, seq_at % 2
    rows = student_hidden.shape[1]
    head_size = head_out.shape[2]
    scale = head_size ** (-0.5) * LOG2E
    length = lengths[0]

    def hop(block, sign):
        route = []
        for z in range(chips):
            for core in range(2):
                way = sign if core == 0 else -sign
                route.append((2 * z + core, 2 * ((z + way) % chips) + core))
        return lax.ppermute(block, "seq", route)

    def other_core(block):
        return lax.ppermute(block, "seq", [(i, i ^ 1) for i in range(seq_count)])

    half_way = chips // 2
    apart = [0, -1]
    for k in range(1, half_way):
        apart += [k, -k - 1]
    apart = jnp.asarray(apart, jnp.int32)

    def places(core):
        return (chip_at + jnp.where(core == 0, apart, -apart)) % chips

    def bias_of(core):
        tokens = (places(core) * 2 + core)[:, None] * rows + jnp.arange(rows, dtype=jnp.int32)
        return jnp.where(tokens < length, 0.0, -1e30)

    normed, *_ = own_rows(
        step_index,
        student_hidden[0],
        student_mod,
        student_out.T,
        noise[0],
        score_stream[0, 0],
        score_in[0],
        score_mod[0],
        (rows,),
    )
    wa = attention_in[0].transpose(1, 0, 2)
    ha = head_out[0].transpose(0, 2, 1)

    up, down = [normed], [normed]
    up.append(hop(up[-1], 1))
    fetched, _ = lax.optimization_barrier((wa, normed))
    wb = other_core(fetched)
    later, *ready = lax.optimization_barrier((normed, *project_first(normed, wa, head_size)))
    down.append(hop(later, -1))
    bias = jnp.concatenate([bias_of(core_at), bias_of(1 - core_at)]).reshape(1, -1)
    up.append(hop(up[-1], 1))

    place = places(core_at)
    qs, owns, fars = [], [], []
    weights, earlier = [wa, wb], ()
    for k in range(half_way):
        q, kv, *kept = project(
            [down[k], up[k + 1]],
            weights,
            head_size,
            keep=k == half_way - 2,
            earlier=earlier,
            ready=() if k else ready,
        )
        weights = kept or weights
        if k == 0:
            begun, kv = lax.optimization_barrier((ha, kv))
            hb = other_core(begun)
        if k + 2 < half_way:
            down[k + 1], q, kv, fars, bias, place = lax.optimization_barrier(
                (down[k + 1], q, kv, fars, bias, place)
            )
            down.append(hop(down[k + 1], -1))
        elif k + 2 == half_way:
            down[k + 1], q, kv, fars, hb = lax.optimization_barrier((down[k + 1], q, kv, fars, hb))
        if k + 3 <= half_way:
            up.append(hop(up[k + 2], 1))
        if k == half_way - 2:
            earlier = (q, kv)
        else:
            qs.append(q)
            owns.append(kv)
            fars.append(other_core(kv))
    terms = attend(place, bias, ha, hb, qs, owns, fars, rows, groups, scale)

    half = terms.shape[2]
    terms = terms.reshape(groups * chips, half, rows)
    same_core = [[g * seq_count + 2 * z + c for g in range(groups) for z in range(chips)] for c in range(2)]
    terms = lax.all_to_all(terms, ("group", "seq"), 0, 0, axis_index_groups=same_core, tiled=True)
    terms = terms.reshape(groups, chips, half, rows)
    gradient = jnp.sum(terms[0], 0) - jnp.sum(terms[1], 0)
    own_places = seq_at * rows + jnp.arange(rows, dtype=jnp.int32)
    return jnp.where((own_places < length)[None, :], gradient, 0.0)[None]


def solution(mesh):
    return jax.shard_map(
        local,
        mesh=mesh,
        in_specs=(
            P("dp", "seq", None),
            P(),
            P(),
            P("group", "dp", "seq", None),
            P("group", None, None),
            P("group", None, None, None),
            P("group", None, None, "seq"),
            P("group", "seq", None, None),
            P("dp"),
            P("dp"),
            P("dp", None, "seq"),
        ),
        out_specs=P("dp", "group", "seq"),
        check_vma=False,
    )
```

```python
import functools

import jax
import jax.numpy as jnp
from jax import lax
from jax.experimental import pallas as pl
from jax.experimental.pallas import tpu as pltpu
from jax.sharding import PartitionSpec as P

epsilon = 1e-06
LOG2E = 1.4426950408889634
MIB = 1 << 20
NT = (((1,), (1,)), ((), ()))
TN = (((0,), (0,)), ((), ()))
NN = (((1,), (0,)), ((), ()))


def dot(a, b, dims):
    return lax.dot_general(a, b, dims, preferred_element_type=jnp.float32)


def layer_norm(values):
    average = jnp.mean(values, -1, keepdims=True)
    centered = values - average
    variance = jnp.mean(centered * centered, -1, keepdims=True)
    return centered * lax.rsqrt(variance + epsilon)


def own_rows_kernel(
    step_ref, hidden_any, mod_any, out_any, noise_any, stream_any, embed_any, table_any, *refs, levels, cuts
):
    normed_refs = refs[: len(cuts)]
    hidden_ref, mod_ref, out_ref, noise_ref, stream_ref, embed_ref, table_ref, sems = refs[len(cuts) :]
    pairs = [
        (hidden_any, hidden_ref),
        (mod_any, mod_ref),
        (out_any, out_ref),
        (noise_any, noise_ref),
        (stream_any, stream_ref),
        (embed_any, embed_ref),
        (table_any.at[step_ref[0]], table_ref),
    ]
    copies = [pltpu.make_async_copy(a, b, sems.at[i]) for i, (a, b) in enumerate(pairs)]
    for copy in copies:
        copy.start()
    copies[0].wait()
    copies[1].wait()
    mod = mod_ref[...]
    student = (
        layer_norm(hidden_ref[...].astype(jnp.float32)) * (1.0 + mod[1:2]) + mod[0:1]
    ).astype(jnp.bfloat16)
    copies[2].wait()
    latent = dot(out_ref[...], student, NT)
    step = jnp.full(latent.shape, step_ref[0], jnp.int32).astype(jnp.float32)
    level = (step + 1.0) / (levels + 1.0)
    copies[3].wait()
    noised = ((1.0 - level) * latent + level * noise_ref[...].astype(jnp.float32)).astype(jnp.bfloat16)
    for copy in copies[4:]:
        copy.wait()
    embedded = stream_ref[...].astype(jnp.float32) + dot(noised, embed_ref[...], TN)
    table = table_ref[...]
    normed = (layer_norm(embedded) * (1.0 + table[1:2]) + table[0:1]).astype(jnp.bfloat16)
    at = 0
    for ref, size in zip(normed_refs, cuts):
        ref[...] = normed[at : at + size]
        at += size


def own_rows(step, hidden, mod, out_t, noise, stream, embed, table, cuts):
    width = hidden.shape[1]
    levels = table.shape[0]
    arrays = (hidden, mod, out_t, noise, stream, embed)
    return pl.pallas_call(
        functools.partial(own_rows_kernel, levels=levels, cuts=cuts),
        in_specs=[pl.BlockSpec(memory_space=pltpu.SMEM)] + [pl.BlockSpec(memory_space=pl.ANY)] * 7,
        out_specs=[pl.BlockSpec(memory_space=pltpu.VMEM)] * len(cuts),
        out_shape=[jax.ShapeDtypeStruct((size, width), jnp.bfloat16) for size in cuts],
        scratch_shapes=[pltpu.VMEM(x.shape, x.dtype) for x in arrays]
        + [pltpu.VMEM((2, width), jnp.float32), pltpu.SemaphoreType.DMA((7,))],
        compiler_params=pltpu.CompilerParams(vmem_limit_bytes=58 * MIB),
        cost_estimate=pl.CostEstimate(flops=2 * 10**8, bytes_accessed=5 * 10**6, transcendentals=0),
        name="own_rows",
    )(step, hidden, mod, out_t, noise, stream, embed, table)


def project_first_kernel(x_ref, w_any, q_ref, kv_ref, w_ref, sems):
    copies = [pltpu.make_async_copy(w_any.at[n], w_ref.at[n], sems.at[n]) for n in range(3)]
    for copy in copies:
        copy.start()
    size = q_ref.shape[2]
    for n in range(3):
        copies[n].wait()
        value = dot(x_ref[...], w_ref[n], NN).astype(jnp.bfloat16)
        for sub in range(2):
            part = value[:, sub * size : (sub + 1) * size]
            if n == 0:
                q_ref[sub] = part
            else:
                kv_ref[2 * (n - 1) + sub] = part


def project_first(x, w, head_size, weight=1):
    rows, width = x.shape
    vmem = pl.BlockSpec(memory_space=pltpu.VMEM)
    return pl.pallas_call(
        project_first_kernel,
        in_specs=[vmem, pl.BlockSpec(memory_space=pl.ANY)],
        out_specs=[vmem] * 2,
        out_shape=[
            jax.ShapeDtypeStruct((2, rows, head_size), jnp.bfloat16),
            jax.ShapeDtypeStruct((4, rows, head_size), jnp.bfloat16),
        ],
        scratch_shapes=[pltpu.VMEM(w.shape, w.dtype), pltpu.SemaphoreType.DMA((3,))],
        compiler_params=pltpu.CompilerParams(vmem_limit_bytes=58 * MIB),
        cost_estimate=pl.CostEstimate(
            flops=weight * 6 * rows * width * w.shape[2], bytes_accessed=weight * 2 * w.size, transcendentals=0
        ),
        name="project_first",
    )(x, w)


def project_kernel(*refs, sizes, fetch, keep, before, ready):
    refs = list(refs)
    x_refs = [refs.pop(0) for _ in sizes]
    w_any = [refs.pop(0) for _ in range(2 if fetch else 1)]
    q_before, kv_before = (refs.pop(0), refs.pop(0)) if before else (None, None)
    done = [(refs.pop(0), refs.pop(0)) for _ in range(ready)]
    q_ref, kv_ref = refs.pop(0), refs.pop(0)
    w_ref = refs.pop(0) if fetch else w_any[0]
    x_buf = refs.pop(0)
    copies, x_copies = [], []
    if fetch:
        sems = refs.pop(0)
        copies = [
            pltpu.make_async_copy(w_any[n // 3].at[n % 3], w_ref.at[n], sems.at[n]) for n in range(6)
        ]
        for copy in copies[:3]:
            copy.start()
    at = 0
    for i, (ref, size) in enumerate(zip(x_refs, sizes)):
        if fetch:
            x_copies.append(pltpu.make_async_copy(ref, x_buf.at[pl.ds(at, size)], sems.at[6 + i]))
            x_copies[-1].start()
        else:
            x_buf[pl.ds(at, size)] = ref[...]
        at += size
    for copy in x_copies:
        copy.wait()
    size = q_ref.shape[2]
    if before:
        q_ref[:, pl.ds(0, before)] = q_before[...]
        kv_ref[:, pl.ds(0, before)] = kv_before[...]
    for n in range(6):
        if fetch:
            copies[n].wait()
            if n + 3 < 6:
                copies[n + 3].start()
        pair, kind = n // 3, n % 3
        skip = sum(sizes[:ready]) if pair == 0 else 0
        here = pl.ds(before + skip, sum(sizes) - skip)
        value = dot(x_buf[pl.ds(skip, sum(sizes) - skip)], w_ref[n], NN).astype(jnp.bfloat16)
        for sub in range(2):
            part = value[:, sub * size : (sub + 1) * size]
            if kind == 0:
                q_ref[2 * pair + sub, here] = part
            else:
                kv_ref[4 * pair + 2 * (kind - 1) + sub, here] = part
    for i, (q_done, kv_done) in enumerate(done):
        q_ref[0:2, pl.ds(sum(sizes[:i]), sizes[i])] = q_done[...]
        kv_ref[0:4, pl.ds(sum(sizes[:i]), sizes[i])] = kv_done[...]


def project(xs, weights, head_size, keep=False, earlier=(), ready=()):
    fetch = len(weights) == 2
    sizes = tuple(x.shape[0] for x in xs)
    width = xs[0].shape[1]
    columns = weights[0].shape[2]
    total = sum(sizes)
    before = earlier[0].shape[1] if earlier else 0
    vmem = pl.BlockSpec(memory_space=pltpu.VMEM)
    out_shape = [
        jax.ShapeDtypeStruct((4, before + total, head_size), jnp.bfloat16),
        jax.ShapeDtypeStruct((8, before + total, head_size), jnp.bfloat16),
    ]
    scratch = [pltpu.VMEM((total, width), jnp.bfloat16)]
    if keep:
        out_shape.append(jax.ShapeDtypeStruct((6, width, columns), jnp.bfloat16))
    elif fetch:
        scratch.insert(0, pltpu.VMEM((6, width, columns), jnp.bfloat16))
    if fetch:
        scratch.append(pltpu.SemaphoreType.DMA((6 + len(xs),)))
    return pl.pallas_call(
        functools.partial(
            project_kernel, sizes=sizes, fetch=fetch, keep=keep, before=before, ready=len(ready) // 2
        ),
        in_specs=[pl.BlockSpec(memory_space=pl.ANY) if fetch else vmem] * (len(xs) + len(weights))
        + [vmem] * (len(earlier) + len(ready)),
        out_specs=[vmem] * len(out_shape),
        out_shape=out_shape,
        scratch_shapes=scratch,
        compiler_params=pltpu.CompilerParams(vmem_limit_bytes=(10 if keep or not fetch else 40) * MIB),
        cost_estimate=pl.CostEstimate(
            flops=2 * total * width * 6 * columns,
            bytes_accessed=12 * width * columns if fetch else 2 * total * width,
            transcendentals=0,
        ),
        name="project_rows",
    )(*xs, *weights, *earlier, *ready)


def attend_kernel(place_ref, bias_ref, ha_ref, hb_ref, *refs, calls, rows, sizes, scale):
    q_refs = refs[:calls]
    own_refs = refs[calls : 2 * calls]
    far_refs = refs[2 * calls : 3 * calls]
    out_ref, q_buf, kv_buf, mix, heads, sems = refs[3 * calls :]
    own = sum(sizes)
    size = q_buf.shape[2]
    pairs = [[], []]
    at = 0
    for i, count in enumerate(sizes):
        here, there = pl.ds(at, count), pl.ds(own + at, count)
        pairs[0].append((q_refs[i], q_buf.at[:, here]))
        for pair in range(2):
            mine, theirs = pl.ds(4 * pair, 4), pl.ds(4 - 4 * pair, 4)
            pairs[pair].append((own_refs[i].at[mine], kv_buf.at[mine, here]))
            pairs[pair].append((far_refs[i].at[theirs], kv_buf.at[mine, there]))
        at += count
    copies = [
        [pltpu.make_async_copy(a, b, sems.at[3 * calls * pair + j]) for j, (a, b) in enumerate(pairs[pair])]
        for pair in range(2)
    ]
    for copy in copies[0] + copies[1]:
        copy.start()
    bias = bias_ref[...]
    for n in range(4):
        if n % 2 == 0:
            for copy in copies[n // 2]:
                copy.wait()
        key = 4 * (n // 2) + n % 2
        scores = dot(q_buf[n], kv_buf[key], NT) * scale + bias
        highest = jnp.max(scores, -1, keepdims=True)
        lifted = jnp.exp2(scores - highest)
        total = jnp.sum(lifted, -1, keepdims=True)
        mixed = dot(lifted.astype(jnp.bfloat16), kv_buf[key + 2], NN) * (1.0 / total)
        mix[:, pl.ds(n * size, size)] = mixed.astype(jnp.bfloat16)
    for n in range(4):
        heads[:, pl.ds(n * size, size)] = (ha_ref if n < 2 else hb_ref)[n % 2]
    half = out_ref.shape[2]
    for j in range(own // rows):
        result = dot(heads[...], mix[pl.ds(j * rows, rows)], NT)
        out_ref[0, place_ref[j]] = result[:half]
        out_ref[1, place_ref[j]] = result[half:]


def attend(place, bias, ha, hb, qs, owns, fars, rows, groups, scale):
    calls = len(qs)
    sizes = tuple(q.shape[1] for q in qs)
    own = sum(sizes)
    head_size = qs[0].shape[2]
    patch = ha.shape[1]
    vmem = pl.BlockSpec(memory_space=pltpu.VMEM)
    return pl.pallas_call(
        functools.partial(attend_kernel, calls=calls, rows=rows, sizes=sizes, scale=scale),
        in_specs=[pl.BlockSpec(memory_space=pltpu.SMEM), vmem, vmem, vmem]
        + [pl.BlockSpec(memory_space=pl.ANY)] * (3 * calls),
        out_specs=vmem,
        out_shape=jax.ShapeDtypeStruct((groups, own // rows, patch // groups, rows), jnp.float32),
        scratch_shapes=[
            pltpu.VMEM((4, own, head_size), jnp.bfloat16),
            pltpu.VMEM((8, 2 * own, head_size), jnp.bfloat16),
            pltpu.VMEM((own, 4 * head_size), jnp.bfloat16),
            pltpu.VMEM((patch, 4 * head_size), jnp.bfloat16),
            pltpu.SemaphoreType.DMA((5 * calls,)),
        ],
        compiler_params=pltpu.CompilerParams(vmem_limit_bytes=26 * MIB),
        cost_estimate=pl.CostEstimate(
            flops=32 * own * own * head_size, bytes_accessed=10**7, transcendentals=8 * own * own
        ),
        name="attend",
    )(place, bias, ha, hb, *qs, *owns, *fars)


def local(
    student_hidden,
    student_mod,
    student_out,
    score_stream,
    score_in,
    score_mod,
    attention_in,
    head_out,
    step_index,
    lengths,
    noise,
):
    groups = lax.axis_size("group")
    seq_count = lax.axis_size("seq")
    chips = seq_count // 2
    seq_at = lax.axis_index("seq")
    chip_at, core_at = seq_at // 2, seq_at % 2
    rows = student_hidden.shape[1]
    head_size = head_out.shape[2]
    scale = head_size ** (-0.5) * LOG2E
    length = lengths[0]

    def hop(block, sign):
        route = []
        for z in range(chips):
            for core in range(2):
                way = sign if core == 0 else -sign
                route.append((2 * z + core, 2 * ((z + way) % chips) + core))
        return lax.ppermute(block, "seq", route)

    def other_core(block):
        return lax.ppermute(block, "seq", [(i, i ^ 1) for i in range(seq_count)])

    apart = [0, -1, 1, -2, 2, -3, 3, -4]
    apart = jnp.asarray(apart, jnp.int32)

    def places(core):
        return (chip_at + jnp.where(core == 0, apart, -apart)) % chips

    def bias_of(core):
        tokens = (places(core) * 2 + core)[:, None] * rows + jnp.arange(rows, dtype=jnp.int32)
        return jnp.where(tokens < length, 0.0, -1e30)

    normed, *_ = own_rows(
        step_index,
        student_hidden[0],
        student_mod,
        student_out.T,
        noise[0],
        score_stream[0, 0],
        score_in[0],
        score_mod[0],
        (rows,),
    )
    wa = attention_in[0].transpose(1, 0, 2)
    ha = head_out[0].transpose(0, 2, 1)

    up, down = [normed], [normed]
    up.append(hop(up[-1], 1))
    fetched, _ = lax.optimization_barrier((wa, normed))
    wb = other_core(fetched)
    later, *ready = lax.optimization_barrier((normed, *project_first(normed, wa, head_size)))
    down.append(hop(later, -1))
    bias = jnp.concatenate([bias_of(core_at), bias_of(1 - core_at)]).reshape(1, -1)
    up.append(hop(up[-1], 1))

    place = places(core_at)
    more = project_first(up[1], wa, head_size, weight=3)
    down[1], bias, place, *more = lax.optimization_barrier((down[1], bias, place, *more))
    down.append(hop(down[1], -1))
    up.append(hop(up[2], 1))

    q, kv = project([normed, up[1], down[1], up[2]], [wa, wb], head_size, ready=[*ready, *more])
    begun, kv = lax.optimization_barrier((ha, kv))
    hb = other_core(begun)
    down[2], q, kv = lax.optimization_barrier((down[2], q, kv))
    down.append(hop(down[2], -1))
    up.append(hop(up[3], 1))
    qs, owns, fars = [q], [kv], [other_core(kv)]
    *earlier, kept = project([down[2], up[3]], [wa, wb], head_size, keep=True)
    down[3], earlier, fars, hb = lax.optimization_barrier((down[3], earlier, fars, hb))
    q, kv = project([down[3], up[4]], [kept], head_size, earlier=earlier)
    qs.append(q)
    owns.append(kv)
    fars.append(other_core(kv))
    terms = attend(place, bias, ha, hb, qs, owns, fars, rows, groups, scale)

    half = terms.shape[2]
    terms = terms.reshape(groups * chips, half, rows)
    same_core = [[g * seq_count + 2 * z + c for g in range(groups) for z in range(chips)] for c in range(2)]
    terms = lax.all_to_all(terms, ("group", "seq"), 0, 0, axis_index_groups=same_core, tiled=True)
    terms = terms.reshape(groups, chips, half, rows)
    gradient = jnp.sum(terms[0], 0) - jnp.sum(terms[1], 0)
    own_places = seq_at * rows + jnp.arange(rows, dtype=jnp.int32)
    return jnp.where((own_places < length)[None, :], gradient, 0.0)[None]


def solution(mesh):
    return jax.shard_map(
        local,
        mesh=mesh,
        in_specs=(
            P("dp", "seq", None),
            P(),
            P(),
            P("group", "dp", "seq", None),
            P("group", None, None),
            P("group", None, None, None),
            P("group", None, None, "seq"),
            P("group", "seq", None, None),
            P("dp"),
            P("dp"),
            P("dp", None, "seq"),
        ),
        out_specs=P("dp", "group", "seq"),
        check_vma=False,
    )
```

```python
import functools

import jax
import jax.numpy as jnp
from jax import lax
from jax.experimental import pallas as pl
from jax.experimental.pallas import tpu as pltpu
from jax.sharding import PartitionSpec as P

epsilon = 1e-06
LOG2E = 1.4426950408889634
MIB = 1 << 20
NT = (((1,), (1,)), ((), ()))
TN = (((0,), (0,)), ((), ()))
NN = (((1,), (0,)), ((), ()))


def dot(a, b, dims):
    return lax.dot_general(a, b, dims, preferred_element_type=jnp.float32)


def layer_norm(values):
    average = jnp.mean(values, -1, keepdims=True)
    centered = values - average
    variance = jnp.mean(centered * centered, -1, keepdims=True)
    return centered * lax.rsqrt(variance + epsilon)


def own_rows_kernel(
    step_ref, hidden_any, mod_any, out_any, noise_any, stream_any, embed_any, table_any, *refs, levels, cuts
):
    normed_refs = refs[: len(cuts)]
    hidden_ref, mod_ref, out_ref, noise_ref, stream_ref, embed_ref, table_ref, sems = refs[len(cuts) :]
    pairs = [
        (hidden_any, hidden_ref),
        (mod_any, mod_ref),
        (out_any, out_ref),
        (noise_any, noise_ref),
        (stream_any, stream_ref),
        (embed_any, embed_ref),
        (table_any.at[step_ref[0]], table_ref),
    ]
    copies = [pltpu.make_async_copy(a, b, sems.at[i]) for i, (a, b) in enumerate(pairs)]
    for copy in copies:
        copy.start()
    copies[0].wait()
    copies[1].wait()
    mod = mod_ref[...]
    student = (
        layer_norm(hidden_ref[...].astype(jnp.float32)) * (1.0 + mod[1:2]) + mod[0:1]
    ).astype(jnp.bfloat16)
    copies[2].wait()
    latent = dot(out_ref[...], student, NT)
    step = jnp.full(latent.shape, step_ref[0], jnp.int32).astype(jnp.float32)
    level = (step + 1.0) / (levels + 1.0)
    copies[3].wait()
    noised = ((1.0 - level) * latent + level * noise_ref[...].astype(jnp.float32)).astype(jnp.bfloat16)
    for copy in copies[4:]:
        copy.wait()
    embedded = stream_ref[...].astype(jnp.float32) + dot(noised, embed_ref[...], TN)
    table = table_ref[...]
    normed = (layer_norm(embedded) * (1.0 + table[1:2]) + table[0:1]).astype(jnp.bfloat16)
    at = 0
    for ref, size in zip(normed_refs, cuts):
        ref[...] = normed[at : at + size]
        at += size


def own_rows(step, hidden, mod, out_t, noise, stream, embed, table, cuts):
    width = hidden.shape[1]
    levels = table.shape[0]
    arrays = (hidden, mod, out_t, noise, stream, embed)
    return pl.pallas_call(
        functools.partial(own_rows_kernel, levels=levels, cuts=cuts),
        in_specs=[pl.BlockSpec(memory_space=pltpu.SMEM)] + [pl.BlockSpec(memory_space=pl.ANY)] * 7,
        out_specs=[pl.BlockSpec(memory_space=pltpu.VMEM)] * len(cuts),
        out_shape=[jax.ShapeDtypeStruct((size, width), jnp.bfloat16) for size in cuts],
        scratch_shapes=[pltpu.VMEM(x.shape, x.dtype) for x in arrays]
        + [pltpu.VMEM((2, width), jnp.float32), pltpu.SemaphoreType.DMA((7,))],
        compiler_params=pltpu.CompilerParams(vmem_limit_bytes=58 * MIB),
        cost_estimate=pl.CostEstimate(flops=2 * 10**8, bytes_accessed=5 * 10**6, transcendentals=0),
        name="own_rows",
    )(step, hidden, mod, out_t, noise, stream, embed, table)


def project_first_kernel(x_ref, w_any, q_ref, kv_ref, w_ref, sems):
    copies = [pltpu.make_async_copy(w_any.at[n], w_ref.at[n], sems.at[n]) for n in range(3)]
    for copy in copies:
        copy.start()
    size = q_ref.shape[2]
    for n in range(3):
        copies[n].wait()
        value = dot(x_ref[...], w_ref[n], NN).astype(jnp.bfloat16)
        for sub in range(2):
            part = value[:, sub * size : (sub + 1) * size]
            if n == 0:
                q_ref[sub] = part
            else:
                kv_ref[2 * (n - 1) + sub] = part


def project_first(x, w, head_size, weight=1):
    rows, width = x.shape
    vmem = pl.BlockSpec(memory_space=pltpu.VMEM)
    return pl.pallas_call(
        project_first_kernel,
        in_specs=[vmem, pl.BlockSpec(memory_space=pl.ANY)],
        out_specs=[vmem] * 2,
        out_shape=[
            jax.ShapeDtypeStruct((2, rows, head_size), jnp.bfloat16),
            jax.ShapeDtypeStruct((4, rows, head_size), jnp.bfloat16),
        ],
        scratch_shapes=[pltpu.VMEM(w.shape, w.dtype), pltpu.SemaphoreType.DMA((3,))],
        compiler_params=pltpu.CompilerParams(vmem_limit_bytes=58 * MIB),
        cost_estimate=pl.CostEstimate(
            flops=weight * 6 * rows * width * w.shape[2], bytes_accessed=weight * 2 * w.size, transcendentals=0
        ),
        name="project_first",
    )(x, w)


def project_kernel(*refs, sizes, fetch, keep, before, ready):
    refs = list(refs)
    x_refs = [refs.pop(0) for _ in sizes]
    w_any = [refs.pop(0) for _ in range(2 if fetch else 1)]
    q_before, kv_before = (refs.pop(0), refs.pop(0)) if before else (None, None)
    done = [(refs.pop(0), refs.pop(0)) for _ in range(ready)]
    q_ref, kv_ref = refs.pop(0), refs.pop(0)
    w_ref = refs.pop(0) if fetch else w_any[0]
    x_buf = refs.pop(0)
    copies, x_copies = [], []
    if fetch:
        sems = refs.pop(0)
        copies = [
            pltpu.make_async_copy(w_any[n // 3].at[n % 3], w_ref.at[n], sems.at[n]) for n in range(6)
        ]
        for copy in copies[:3]:
            copy.start()
    at = 0
    for i, (ref, size) in enumerate(zip(x_refs, sizes)):
        if fetch:
            x_copies.append(pltpu.make_async_copy(ref, x_buf.at[pl.ds(at, size)], sems.at[6 + i]))
            x_copies[-1].start()
        else:
            x_buf[pl.ds(at, size)] = ref[...]
        at += size
    for copy in x_copies:
        copy.wait()
    size = q_ref.shape[2]
    if before:
        q_ref[:, pl.ds(0, before)] = q_before[...]
        kv_ref[:, pl.ds(0, before)] = kv_before[...]
    for n in range(6):
        if fetch:
            copies[n].wait()
            if n + 3 < 6:
                copies[n + 3].start()
        pair, kind = n // 3, n % 3
        skip = sum(sizes[:ready]) if pair == 0 else 0
        here = pl.ds(before + skip, sum(sizes) - skip)
        value = dot(x_buf[pl.ds(skip, sum(sizes) - skip)], w_ref[n], NN).astype(jnp.bfloat16)
        for sub in range(2):
            part = value[:, sub * size : (sub + 1) * size]
            if kind == 0:
                q_ref[2 * pair + sub, here] = part
            else:
                kv_ref[4 * pair + 2 * (kind - 1) + sub, here] = part
    for i, (q_done, kv_done) in enumerate(done):
        q_ref[0:2, pl.ds(sum(sizes[:i]), sizes[i])] = q_done[...]
        kv_ref[0:4, pl.ds(sum(sizes[:i]), sizes[i])] = kv_done[...]


def project(xs, weights, head_size, keep=False, earlier=(), ready=()):
    fetch = len(weights) == 2
    sizes = tuple(x.shape[0] for x in xs)
    width = xs[0].shape[1]
    columns = weights[0].shape[2]
    total = sum(sizes)
    before = earlier[0].shape[1] if earlier else 0
    vmem = pl.BlockSpec(memory_space=pltpu.VMEM)
    out_shape = [
        jax.ShapeDtypeStruct((4, before + total, head_size), jnp.bfloat16),
        jax.ShapeDtypeStruct((8, before + total, head_size), jnp.bfloat16),
    ]
    scratch = [pltpu.VMEM((total, width), jnp.bfloat16)]
    if keep:
        out_shape.append(jax.ShapeDtypeStruct((6, width, columns), jnp.bfloat16))
    elif fetch:
        scratch.insert(0, pltpu.VMEM((6, width, columns), jnp.bfloat16))
    if fetch:
        scratch.append(pltpu.SemaphoreType.DMA((6 + len(xs),)))
    return pl.pallas_call(
        functools.partial(
            project_kernel, sizes=sizes, fetch=fetch, keep=keep, before=before, ready=len(ready) // 2
        ),
        in_specs=[pl.BlockSpec(memory_space=pl.ANY) if fetch else vmem] * (len(xs) + len(weights))
        + [vmem] * (len(earlier) + len(ready)),
        out_specs=[vmem] * len(out_shape),
        out_shape=out_shape,
        scratch_shapes=scratch,
        compiler_params=pltpu.CompilerParams(vmem_limit_bytes=(10 if keep or not fetch else 58) * MIB),
        cost_estimate=pl.CostEstimate(
            flops=2 * total * width * 6 * columns,
            bytes_accessed=12 * width * columns if fetch else 2 * total * width,
            transcendentals=0,
        ),
        name="project_rows",
    )(*xs, *weights, *earlier, *ready)


def attend_kernel(place_ref, bias_ref, ha_ref, hb_ref, *refs, calls, rows, sizes, scale):
    q_refs = refs[:calls]
    own_refs = refs[calls : 2 * calls]
    far_refs = refs[2 * calls : 3 * calls]
    out_ref, q_buf, kv_buf, mix, heads, sems = refs[3 * calls :]
    own = sum(sizes)
    size = q_buf.shape[2]
    pairs = [[], []]
    at = 0
    for i, count in enumerate(sizes):
        here, there = pl.ds(at, count), pl.ds(own + at, count)
        pairs[0].append((q_refs[i], q_buf.at[:, here]))
        for pair in range(2):
            mine, theirs = pl.ds(4 * pair, 4), pl.ds(4 - 4 * pair, 4)
            pairs[pair].append((own_refs[i].at[mine], kv_buf.at[mine, here]))
            pairs[pair].append((far_refs[i].at[theirs], kv_buf.at[mine, there]))
        at += count
    copies = [
        [pltpu.make_async_copy(a, b, sems.at[3 * calls * pair + j]) for j, (a, b) in enumerate(pairs[pair])]
        for pair in range(2)
    ]
    for copy in copies[0] + copies[1]:
        copy.start()
    bias = bias_ref[...]
    for n in range(4):
        if n % 2 == 0:
            for copy in copies[n // 2]:
                copy.wait()
        key = 4 * (n // 2) + n % 2
        scores = dot(q_buf[n], kv_buf[key], NT) * scale + bias
        highest = jnp.max(scores, -1, keepdims=True)
        lifted = jnp.exp2(scores - highest)
        total = jnp.sum(lifted, -1, keepdims=True)
        mixed = dot(lifted.astype(jnp.bfloat16), kv_buf[key + 2], NN) * (1.0 / total)
        mix[:, pl.ds(n * size, size)] = mixed.astype(jnp.bfloat16)
    for n in range(4):
        heads[:, pl.ds(n * size, size)] = (ha_ref if n < 2 else hb_ref)[n % 2]
    half = out_ref.shape[2]
    for j in range(own // rows):
        result = dot(heads[...], mix[pl.ds(j * rows, rows)], NT)
        out_ref[0, place_ref[j]] = result[:half]
        out_ref[1, place_ref[j]] = result[half:]


def attend(place, bias, ha, hb, qs, owns, fars, rows, groups, scale):
    calls = len(qs)
    sizes = tuple(q.shape[1] for q in qs)
    own = sum(sizes)
    head_size = qs[0].shape[2]
    patch = ha.shape[1]
    vmem = pl.BlockSpec(memory_space=pltpu.VMEM)
    return pl.pallas_call(
        functools.partial(attend_kernel, calls=calls, rows=rows, sizes=sizes, scale=scale),
        in_specs=[pl.BlockSpec(memory_space=pltpu.SMEM), vmem, vmem, vmem]
        + [pl.BlockSpec(memory_space=pl.ANY)] * (3 * calls),
        out_specs=vmem,
        out_shape=jax.ShapeDtypeStruct((groups, own // rows, patch // groups, rows), jnp.float32),
        scratch_shapes=[
            pltpu.VMEM((4, own, head_size), jnp.bfloat16),
            pltpu.VMEM((8, 2 * own, head_size), jnp.bfloat16),
            pltpu.VMEM((own, 4 * head_size), jnp.bfloat16),
            pltpu.VMEM((patch, 4 * head_size), jnp.bfloat16),
            pltpu.SemaphoreType.DMA((5 * calls,)),
        ],
        compiler_params=pltpu.CompilerParams(vmem_limit_bytes=26 * MIB),
        cost_estimate=pl.CostEstimate(
            flops=32 * own * own * head_size, bytes_accessed=10**7, transcendentals=8 * own * own
        ),
        name="attend",
    )(place, bias, ha, hb, *qs, *owns, *fars)


def local(
    student_hidden,
    student_mod,
    student_out,
    score_stream,
    score_in,
    score_mod,
    attention_in,
    head_out,
    step_index,
    lengths,
    noise,
):
    groups = lax.axis_size("group")
    seq_count = lax.axis_size("seq")
    chips = seq_count // 2
    seq_at = lax.axis_index("seq")
    chip_at, core_at = seq_at // 2, seq_at % 2
    rows = student_hidden.shape[1]
    head_size = head_out.shape[2]
    scale = head_size ** (-0.5) * LOG2E
    length = lengths[0]

    def hop(block, sign):
        route = []
        for z in range(chips):
            for core in range(2):
                way = sign if core == 0 else -sign
                route.append((2 * z + core, 2 * ((z + way) % chips) + core))
        return lax.ppermute(block, "seq", route)

    def other_core(block):
        return lax.ppermute(block, "seq", [(i, i ^ 1) for i in range(seq_count)])

    apart = [0, -1, 1, -2, 2, -3, 3, -4]
    apart = jnp.asarray(apart, jnp.int32)

    def places(core):
        return (chip_at + jnp.where(core == 0, apart, -apart)) % chips

    def bias_of(core):
        tokens = (places(core) * 2 + core)[:, None] * rows + jnp.arange(rows, dtype=jnp.int32)
        return jnp.where(tokens < length, 0.0, -1e30)

    normed, *_ = own_rows(
        step_index,
        student_hidden[0],
        student_mod,
        student_out.T,
        noise[0],
        score_stream[0, 0],
        score_in[0],
        score_mod[0],
        (rows,),
    )
    wa = attention_in[0].transpose(1, 0, 2)
    ha = head_out[0].transpose(0, 2, 1)

    up, down = [normed], [normed]
    up.append(hop(up[-1], 1))
    fetched, _ = lax.optimization_barrier((wa, normed))
    wb = other_core(fetched)
    later, *ready = lax.optimization_barrier((normed, *project_first(normed, wa, head_size)))
    down.append(hop(later, -1))
    bias = jnp.concatenate([bias_of(core_at), bias_of(1 - core_at)]).reshape(1, -1)
    up.append(hop(up[-1], 1))

    place = places(core_at)
    more = project_first(up[1], wa, head_size, weight=3)
    down[1], bias, place, *more = lax.optimization_barrier((down[1], bias, place, *more))
    down.append(hop(down[1], -1))
    up.append(hop(up[2], 1))

    q, kv = project([normed, up[1], down[1], up[2]], [wa, wb], head_size, ready=[*ready, *more])
    begun, kv = lax.optimization_barrier((ha, kv))
    hb = other_core(begun)
    down[2], q, kv = lax.optimization_barrier((down[2], q, kv))
    down.append(hop(down[2], -1))
    up.append(hop(up[3], 1))
    qs, owns, fars = [q], [kv], [other_core(kv)]
    *earlier, kept = project([down[2], up[3]], [wa, wb], head_size, keep=True)
    down[3], earlier, fars, hb = lax.optimization_barrier((down[3], earlier, fars, hb))
    q, kv = project([down[3], up[4]], [kept], head_size, earlier=earlier)
    qs.append(q)
    owns.append(kv)
    fars.append(other_core(kv))
    terms = attend(place, bias, ha, hb, qs, owns, fars, rows, groups, scale)

    half = terms.shape[2]
    terms = terms.reshape(groups * chips, half, rows)
    same_core = [[g * seq_count + 2 * z + c for g in range(groups) for z in range(chips)] for c in range(2)]
    terms = lax.all_to_all(terms, ("group", "seq"), 0, 0, axis_index_groups=same_core, tiled=True)
    terms = terms.reshape(groups, chips, half, rows)
    gradient = jnp.sum(terms[0], 0) - jnp.sum(terms[1], 0)
    own_places = seq_at * rows + jnp.arange(rows, dtype=jnp.int32)
    return jnp.where((own_places < length)[None, :], gradient, 0.0)[None]


def solution(mesh):
    return jax.shard_map(
        local,
        mesh=mesh,
        in_specs=(
            P("dp", "seq", None),
            P(),
            P(),
            P("group", "dp", "seq", None),
            P("group", None, None),
            P("group", None, None, None),
            P("group", None, None, "seq"),
            P("group", "seq", None, None),
            P("dp"),
            P("dp"),
            P("dp", None, "seq"),
        ),
        out_specs=P("dp", "group", "seq"),
        check_vma=False,
    )
```
